128 devices in a mesh: dp: 16 (over x, z), tensor: 8 (over y, core).
Axes of the slice: x: 4, y: 4, z: 4, core: 2. Of those that a mesh axis runs over, the one named last changes fastest.
Arguments:
- queries: bfloat16 [16, 512, 8192], P('dp', None, 'tensor'), may hold values from -8 to 8
- new_keys: bfloat16 [16, 512, 512], P('dp', None, 'tensor'), may hold values from -8 to 8
- new_values: bfloat16 [16, 512, 512], P('dp', None, 'tensor'), may hold values from -6 to 6
- key_cache: bfloat16 [1024, 128, 512], P('dp', None, 'tensor'), may hold values from -8 to 8
- value_cache: bfloat16 [1024, 128, 512], P('dp', None, 'tensor'), may hold values from -6 to 6
- page_owner: int32 [32, 8, 1], replicated, may hold values from 0 to 15; in each aligned block of 16 rows (0 to 15, 16 to 31, ..., all dimensions but the last counted through in order) at most 4 rows name the same one
- page_slot: int32 [32, 8], replicated, may hold values from 0 to 63
- tile_req: int32 [96], replicated, may hold values from 0 to 15, as said below
- tile_node: int32 [96], replicated, may hold values from 0 to 31, as said below
- suffix_len: int32 [16], P('dp'), may hold values from 1 to 512, 6144 in all
Outputs:
- attended: bfloat16 [16, 512, 8192], P('dp', None, 'tensor')
The draws below stay inside these ranges and needn't reach their ends.
Inputs may be any that keep to these rules, and one draw needn't show every extreme that they name: `page_owner`: in each aligned block of 16 entries (the nodes kept by one index of dp) no owner appears more than 4 times. `tile_req`: the 6 tiles of one index of dp, positions e * 6 onward, name different requests. `tile_node`: tile i names a node of index i // 6 of dp, one of i // 6 * 2 to i // 6 * 2 + 1, and every node is named by some tile.
All inputs are finite; a program needn't handle non-finite values. No bound on the sum of `suffix_len` on one device may be relied on, other than what follows from the above.
Results may differ from the reference program's by a relative error of at most 0.0038.
Values may be sent and summed in bfloat16 or wider, within the bound.
A program may use at most 128 MiB of HBM per device.

```python
import math
import jax
import jax.numpy as jnp
import numpy as np
from jax import lax

QH = 64
KVH = 4
HD = 128
SUF = 512
TILE_DEV = 6
NODE_DEV = 2
PAGES_NODE = 8
PAGE = 128
PAGES_DEV = 64
CAP = 4
REQS = 16
NODES = 32
PAGES = 1024
TILES = 96
N_DP = 16


def draw_queries(key, part):
    key = jax.random.fold_in(key, 3)
    noise_key = jax.random.fold_in(key, 0)
    feature_rows = jnp.clip(jax.random.normal(noise_key, (REQS, SUF, QH, HD), jnp.float32), -6.0, 6.0)
    return feature_rows.reshape(REQS, SUF, QH * HD).astype(jnp.bfloat16)


def draw_new_keys(key, part):
    key = jax.random.fold_in(key, 5)
    noise_key = jax.random.fold_in(key, 0)
    feature_rows = jnp.clip(jax.random.normal(noise_key, (REQS, SUF, KVH, HD), jnp.float32), -6.0, 6.0)
    return feature_rows.reshape(REQS, SUF, KVH * HD).astype(jnp.bfloat16)


def draw_key_cache(key, part):
    key = jax.random.fold_in(key, 7)
    noise_key = jax.random.fold_in(key, 0)
    feature_rows = jnp.clip(jax.random.normal(noise_key, (PAGES, PAGE, KVH, HD), jnp.float32), -6.0, 6.0)
    return feature_rows.reshape(PAGES, PAGE, KVH * HD).astype(jnp.bfloat16)


def draw_tile_req(key, part):
    key = jax.random.fold_in(key, 11)
    heat_key, noise_key, order_key = jax.random.split(key, 3)
    heat_level = jax.random.randint(heat_key, (REQS,), 0, 4)
    noise_draw = jax.random.randint(noise_key, (N_DP, REQS), 0, 4)
    shuffled = jax.random.permutation(order_key, REQS)
    ranking = (heat_level[None, :] * 2 + noise_draw) * REQS + shuffled[None, :]
    chosen = lax.top_k(ranking, TILE_DEV)[1]
    return chosen.reshape(TILES).astype(jnp.int32)


def draw_tile_node(key, part):
    key = jax.random.fold_in(key, 13)
    offset = jax.random.randint(key, (N_DP, 1), 0, NODE_DEV)
    local_node = (offset + jnp.arange(TILE_DEV)[None, :]) % NODE_DEV
    holder = jnp.arange(N_DP)[:, None] * NODE_DEV
    return (holder + local_node).reshape(TILES).astype(jnp.int32)


def touch_ends(drawn, own_key, least, largest):
    shape = drawn.shape
    place = [jax.random.randint(jax.random.fold_in(own_key, axis), (), 0, shape[axis]) for axis in range(len(shape))]
    drawn = drawn.at[tuple(place)].set(least)
    longest = shape.index(max(shape))
    place[longest] = (place[longest] + 1) % shape[longest]
    return drawn.at[tuple(place)].set(largest)


def steps_of(stream_key, shape, shards, low, largest):
    level, own = 1.0, jax.random.fold_in(stream_key, 6)
    for dim, parts in shards:
        steps = jnp.exp(jax.random.uniform(jax.random.fold_in(own, dim), (parts,), jnp.float32, low / len(shards), largest / len(shards)))
        level = level * jnp.repeat(steps, shape[dim] // parts).reshape([-1 if axis == dim else 1 for axis in range(len(shape))])
    return level


def length_profile(count, total, limit, lean):
    loads = [(1 << 20) // math.isqrt(standing ** lean) + 1 for standing in range(2, count + 1)]
    rest, given = total - limit - (count - 1), [1] * (count - 1)
    while rest > 0:
        candidates = [i for i in range(count - 1) if given[i] < limit]
        whole, remaining = sum([loads[i] for i in candidates]), rest
        for i in candidates:
            addition = min(limit - given[i], max(1, remaining * loads[i] // whole), rest)
            given[i] = given[i] + addition
            rest = rest - addition
    return np.array([limit] + given)


def ragged(own_key, number_of, total, most, lean):
    if number_of == 2:
        one = jax.random.randint(own_key, (), max(1, total - most), min(most, total - 1) + 1)
        return jnp.stack([one, total - one])
    sizes = jnp.asarray(length_profile(number_of, total, most, lean), jnp.int32)
    twos = (number_of - 1) // 2
    donor, receiver = sizes[1:1 + 2 * twos:2], sizes[2:2 + 2 * twos:2]
    slack = jnp.minimum(donor - 1, most - receiver)
    shifted = jax.random.randint(jax.random.fold_in(own_key, 1), (twos,), 0, 1 << 20) % (slack + 1)
    sizes = sizes.at[1:1 + 2 * twos:2].set(donor - shifted).at[2:2 + 2 * twos:2].set(receiver + shifted)
    return sizes[jax.random.permutation(jax.random.fold_in(own_key, 2), number_of)]


def shared_out(key, own, number, rows, amount, top, reach, slope):
    order = jax.random.permutation(key, amount)
    packed, usual = portions_of(amount, rows * top, reach, slope, True), portions_of(amount, rows * top, reach, slope, False)
    places = jnp.arange(amount)

    def named(tallies, offset_by):
        used = int((tallies > 0).sum())
        fixed = max(1, used // 4)
        shifted = fixed + (places - fixed + offset_by * (used - fixed)) % max(1, amount - fixed)
        return jnp.zeros((amount,), jnp.int32).at[order[jnp.where(places < fixed, places, shifted)]].set(jnp.asarray(tallies, jnp.int32))

    tallies = jnp.where(number % 4 == 0, named(packed, number // 4), named(usual, number - number // 4 - 1))
    mixed = jax.random.permutation(jax.random.fold_in(own, 3), amount)
    donor, receiver = mixed[0:amount // 2 * 2:2], mixed[1:amount // 2 * 2:2]
    slack = jnp.minimum(tallies[donor] - 1, reach - tallies[receiver]) // 2
    slack = jnp.where((donor == order[0]) | (receiver == order[0]) | (tallies[receiver] == 0), 0, jnp.maximum(slack, 0))
    shifted = jax.random.randint(jax.random.fold_in(own, 4), (amount // 2,), 0, 1 << 20) % (slack + 1)
    tallies = tallies.at[donor].add(-shifted).at[receiver].add(shifted)
    labels = jnp.searchsorted(jnp.cumsum(tallies), jnp.arange(rows * top), side="right").astype(jnp.int32)
    table = labels.reshape(top, rows).T
    table = table[jax.random.permutation(jax.random.fold_in(own, 1), rows)]
    offset_by = jax.random.randint(jax.random.fold_in(own, 2), (rows, 1), 0, top)
    return jnp.take_along_axis(table, (jnp.arange(top)[None, :] + offset_by) % top, axis=1)


def portions_of(count, total, most, slope, full):
    loads = [(1 << 20) // math.isqrt(rank ** slope) + 1 for rank in range(1, count + 1)]
    largest = most if full else min(most, max(-(-total // count), total * loads[0] // sum(loads)))
    least = 1 if total - largest >= count - 1 else 0
    counts, spare = [largest] + [least] * (count - 1), total - largest - least * (count - 1)
    while spare > 0:
        free = [i for i in range(1, count) if counts[i] < largest] or [i for i in range(1, count) if counts[i] < most]
        mass, budget = sum([loads[i] for i in free]), spare
        for i in free:
            more = min(most - counts[i], max(1, budget * loads[i] // mass), spare)
            counts[i] = counts[i] + more
            spare = spare - more
    return np.array(counts)


def gaussian(own_key, shape, deviation, reach, cuts=(), dtype=jnp.bfloat16):
    level = steps_of(own_key, shape, cuts, -0.22, 0.18) if cuts else 1.0
    array = jax.random.normal(own_key, shape, jnp.float32) * deviation * level
    return jnp.minimum(jnp.maximum(array, -reach), reach).astype(dtype)


def setup_inputs(seed: int = 0) -> dict:
    splits = jax.random.split(jax.random.key(seed), 11)
    queries = draw_queries(jax.random.fold_in(splits[10], 71), 0)
    new_keys = draw_new_keys(jax.random.fold_in(splits[10], 71), 0)
    new_values = gaussian(splits[2], (REQS, SUF, KVH * HD), 1.0, 6.0, ((0, 16), (2, 8)))
    key_cache = draw_key_cache(jax.random.fold_in(splits[10], 71), 0)
    value_cache = gaussian(splits[4], (PAGES, PAGE, KVH * HD), 1.0, 6.0, ((0, 16), (2, 8)))
    page_owner_keys = jax.random.split(jax.random.fold_in(splits[5], 1), NODES * PAGES_NODE // (NODE_DEV * PAGES_NODE))
    page_owner_turns = jax.random.permutation(jax.random.fold_in(splits[5], 3), NODES * PAGES_NODE // (NODE_DEV * PAGES_NODE))
    page_owner = jax.vmap(lambda own, number: shared_out(jax.random.fold_in(splits[5], 2), own, number, NODE_DEV * PAGES_NODE, N_DP, 1, CAP, 2))(page_owner_keys, page_owner_turns).reshape((NODES, PAGES_NODE, 1))
    page_slot = touch_ends(jax.random.randint(splits[6], (NODES, PAGES_NODE), 0, PAGES_DEV), jax.random.fold_in(splits[6], 1), 0, PAGES_DEV - 1).astype(jnp.int32)
    tile_req = draw_tile_req(jax.random.fold_in(splits[10], 71), 0)
    tile_node = draw_tile_node(jax.random.fold_in(splits[10], 71), 0)
    suffix_len = ragged(splits[9], REQS, REQS * SUF * 3 // 4, SUF, 1).astype(jnp.int32)
    return {"queries": queries, "new_keys": new_keys, "new_values": new_values, "key_cache": key_cache, "value_cache": value_cache, "page_owner": page_owner, "page_slot": page_slot, "tile_req": tile_req, "tile_node": tile_node, "suffix_len": suffix_len}


FLOOR_SCORE = -1e+30

def node_rows_of(cache, page_owner, page_slot, node_id):
    page_ids = (page_owner[node_id, :, 0] * PAGES_DEV + page_slot[node_id]).astype(jnp.int32)
    page_rows = jnp.take(cache, page_ids, axis=0)
    return page_rows.reshape(PAGES_NODE * PAGE, KVH, HD).astype(jnp.float32)

def reference(queries, new_keys, new_values, key_cache, value_cache, page_owner, page_slot, tile_req, tile_node, suffix_len):
    softmax_scale = 1.0 / math.sqrt(HD)
    group_size = QH // KVH

    def tile_part(tile_index):
        request = tile_req[tile_index]
        node_id = tile_node[tile_index]
        query_rows = queries[request].astype(jnp.float32).reshape(SUF, KVH, group_size, HD)
        key_rows = node_rows_of(key_cache, page_owner, page_slot, node_id)
        value_rows = node_rows_of(value_cache, page_owner, page_slot, node_id)
        score = jnp.einsum('sgrd,kgd->grsk', query_rows, key_rows) * softmax_scale
        row_max = lax.optimization_barrier(jnp.max(score, axis=-1))
        weight = jnp.exp(score - row_max[..., None])
        row_sum = lax.optimization_barrier(jnp.sum(weight, axis=-1))
        rounded = lax.optimization_barrier(weight.astype(jnp.bfloat16)).astype(jnp.float32)
        mixed = jnp.einsum('grsk,kgd->sgrd', rounded, value_rows)
        return (row_max.reshape(QH, SUF).T, row_sum.reshape(QH, SUF).T, mixed.reshape(SUF, QH, HD).astype(jnp.bfloat16))

    def suffix_part(request):
        query_rows = queries[request].astype(jnp.float32).reshape(SUF, KVH, group_size, HD)
        key_rows = new_keys[request].astype(jnp.float32).reshape(SUF, KVH, HD)
        value_rows = new_values[request].astype(jnp.float32).reshape(SUF, KVH, HD)
        score = jnp.einsum('igrd,jgd->grij', query_rows, key_rows) * softmax_scale
        position = jnp.arange(SUF)
        allowed = (position[None, :] <= position[:, None]) & (position[None, :] < suffix_len[request])
        score = jnp.where(allowed, score, FLOOR_SCORE)
        row_max = lax.optimization_barrier(jnp.max(score, axis=-1))
        weight = jnp.exp(score - row_max[..., None])
        row_sum = lax.optimization_barrier(jnp.sum(weight, axis=-1))
        rounded = lax.optimization_barrier(weight.astype(jnp.bfloat16)).astype(jnp.float32)
        mixed = jnp.einsum('grij,jgd->igrd', rounded, value_rows)
        return (row_max.reshape(QH, SUF).T, row_sum.reshape(QH, SUF).T, mixed.reshape(SUF, QH, HD))
    tile_max, tile_sum, tile_out = lax.map(tile_part, jnp.arange(TILES))
    self_max, self_sum, self_out = lax.map(suffix_part, jnp.arange(REQS))
    global_max = jnp.maximum(self_max, jax.ops.segment_max(tile_max, tile_req, num_segments=REQS))
    tile_factor = jnp.exp(tile_max - global_max[tile_req])
    self_factor = jnp.exp(self_max - global_max)
    row_sum = self_sum * self_factor + jax.ops.segment_sum(tile_sum * tile_factor, tile_req, num_segments=REQS)
    mixed = self_out * self_factor[..., None] + jax.ops.segment_sum(tile_out.astype(jnp.float32) * tile_factor[..., None], tile_req, num_segments=REQS)
    is_valid = jnp.arange(SUF)[None, :] < suffix_len[:, None]
    result = jnp.where(is_valid[:, :, None, None], mixed / row_sum[..., None], 0.0)
    return result.reshape(REQS, SUF, QH * HD).astype(jnp.bfloat16)
```

```python
import functools
import math

import jax
import jax.numpy as jnp
from jax import lax
from jax.experimental import pallas as pl
from jax.experimental.pallas import tpu as pltpu
from jax.sharding import PartitionSpec as P

HD = 128
CAP = 4
SIDE = 4
FLOOR_SCORE = -1e30
SCALE = 1.0 / math.sqrt(HD)
LOG2E = math.log2(math.e)
MESH = pl.DeviceIdType.MESH
MIB = 1 << 20


def from_partner(block):
    return lax.ppermute(block, "tensor", [(i, i ^ 1) for i in range(lax.axis_size("tensor"))])


def neighbour(me, axis, step):
    slow, fast = me // SIDE, me % SIDE
    if axis == 0:
        return lax.rem(slow + step, SIDE) * SIDE + fast
    return slow * SIDE + lax.rem(fast + step, SIDE)


def exchange_kernel(axis, with_small, *refs):
    if with_small:
        x_ref, y_ref, o_ref, oy_ref, mid, rel, s1, r1, s2, r2, lsem, ys, yr = refs
    else:
        x_ref, o_ref, mid, rel, s1, r1, s2, r2, lsem = refs
    me, t = lax.axis_index("dp"), lax.axis_index("tensor")
    place = (me // SIDE, me % SIDE)
    n = x_ref.shape[2 + axis] // 4

    def crd(a, k):
        return lax.rem(place[a] + k, SIDE)

    def cut(ref, start, size):
        return ref.at[:, start : start + size, :] if axis == 0 else ref.at[:, :, start : start + size]

    def quarter(ref, half, sub):
        return cut(ref, half * 2 * n, 2 * n) if sub is None else cut(ref, (half * 2 + sub) * n, n)

    def part(ref, sub):
        return ref if sub is None else cut(ref, sub * n, n)

    barrier = pltpu.get_barrier_semaphore()
    if with_small:
        for k in range(1, 16):
            pl.semaphore_signal(barrier, inc=1, device_id=(lax.rem(me + k, 16), t), device_id_type=MESH)
        pl.semaphore_wait(barrier, 15)
    else:
        for a in (0, 1):
            for k in (1, 3):
                pl.semaphore_signal(barrier, inc=1, device_id=(neighbour(me, a, k), t), device_id_type=MESH)
        pl.semaphore_wait(barrier, 4)

    def copy(src, dst, ss, rs, a, k):
        c = pltpu.make_async_remote_copy(
            src_ref=src, dst_ref=dst, send_sem=ss, recv_sem=rs, device_id=(neighbour(me, a, k), t), device_id_type=MESH
        )
        c.start()
        return c

    def phase(source, target, ss, rs, swap, relay):
        far, near = [], []
        for h in (0, 1):
            a = 1 - h if swap else h
            for j, k in ((0, 1), (1, 3)):
                far.append((h, j, k, copy(source(h, crd(a, 2), j), relay.at[h, j], ss.at[h, 0, j], rs.at[h, 0, j], a, k)))
            for j, k in ((0, 1), (1, 3)):
                near.append(copy(source(h, crd(a, k), None), target(h, crd(a, 0), None), ss.at[h, 1, j], rs.at[h, 1, j], a, k))
        for h, j, k, c in far:
            a = 1 - h if swap else h
            c.wait_recv()
            near.append(copy(relay.at[h, j], target(h, crd(a, 4 - k), j), ss.at[h, 2, j], rs.at[h, 2, j], a, k))
        for _, _, _, c in far:
            c.wait_send()
        return near

    def slab(ref, h, i):
        return ref.at[i] if h == 0 else ref.at[:, i]

    small = []
    if with_small:
        for k in range(1, 16):
            d = lax.rem(me + k, 16)
            c = pltpu.make_async_remote_copy(
                src_ref=y_ref.at[d], dst_ref=oy_ref.at[me], send_sem=ys.at[k], recv_sem=yr.at[k], device_id=(d, t), device_id_type=MESH
            )
            c.start()
            small.append(c)
        c = pltpu.make_async_copy(y_ref.at[me], oy_ref.at[me], ys.at[0])
        c.start()
        small.append(c)
    own = []
    for h in (0, 1):
        c = pltpu.make_async_copy(quarter(slab(x_ref, h, crd(h, 0)), h, None), mid.at[h, crd(h, 0)], lsem.at[h])
        c.start()
        own.append(c)
    flying = phase(
        lambda h, i, sub: quarter(slab(x_ref, h, i), h, sub), lambda h, i, sub: part(mid.at[h, i], sub), s1, r1, False, rel.at[0]
    )
    for c in own + flying:
        c.wait()

    def landing(h, b, sub):
        return quarter(o_ref.at[:, b] if h == 0 else o_ref.at[b], h, sub)

    own = []
    for h in (0, 1):
        b = crd(1 - h, 0)
        c = pltpu.make_async_copy(mid.at[h, :, b], landing(h, b, None), lsem.at[2 + h])
        c.start()
        own.append(c)
    flying = phase(lambda h, i, sub: part(mid.at[h, :, i], sub), landing, s2, r2, True, rel.at[1])
    for c in own + flying + small:
        c.wait()


def exchange(x, axis, collective_id, small=None):
    rows, lanes = x.shape[2:]
    half = (rows // 2, lanes) if axis == 0 else (rows, lanes // 2)
    sub = (rows // 4, lanes) if axis == 0 else (rows, lanes // 4)
    anywhere = pl.BlockSpec(memory_space=pl.ANY)
    args = (x,) if small is None else (x, small)
    scratch = [
        pltpu.VMEM((2, SIDE, SIDE) + half, x.dtype),
        pltpu.VMEM((2, 2, 2, SIDE) + sub, x.dtype),
        *[pltpu.SemaphoreType.DMA((2, 3, 2)) for _ in range(4)],
        pltpu.SemaphoreType.DMA((4,)),
    ]
    if small is not None:
        scratch += [pltpu.SemaphoreType.DMA((16,)), pltpu.SemaphoreType.DMA((16,))]
    out = pl.pallas_call(
        functools.partial(exchange_kernel, axis, small is not None),
        out_shape=[jax.ShapeDtypeStruct(a.shape, a.dtype) for a in args],
        in_specs=[anywhere] * len(args),
        out_specs=[anywhere] * len(args),
        scratch_shapes=scratch,
        compiler_params=pltpu.CompilerParams(collective_id=collective_id, has_side_effects=True, vmem_limit_bytes=32 * MIB),
    )(*args)
    return out[0] if small is None else out


def tiles_kernel(with_compute, tile_ref, slot_ref, own_ref, q_ref, o_ref, lse_ref, *scratch):
    blocks = scratch[:16]
    q_cols, k_rows, v_cols, part, part_max, acc, acc_max, ss, rs, ps, pr, lsem = scratch[16:]
    me, t = lax.axis_index("dp"), lax.axis_index("tensor")
    core = lax.rem(t, 2)
    mate = t + 1 - 2 * core
    place = (me // SIDE, me % SIDE)

    barrier = pltpu.get_barrier_semaphore()
    for a in (0, 1):
        for k in (1, 3):
            pl.semaphore_signal(barrier, inc=1, device_id=(neighbour(me, a, k), t), device_id_type=MESH)
    pl.semaphore_signal(barrier, inc=1, device_id=(me, mate), device_id_type=MESH)
    pl.semaphore_wait(barrier, 5)

    def number(h, i, j):
        i, j = i % SIDE, j % SIDE
        return i * SIDE + j if h == 0 else j * SIDE + i

    def block(h, i, j, kind):
        ref = blocks[number(h, i, j)].at[h, core]
        return ref if kind is None else ref.at[kind]

    sends, recvs, mates = [], {}, {}

    def send(h, i, j, first, k, kind=None):
        to = (i - k, j) if first else (i, j - k)
        a = h if first else 1 - h
        w = 0 if kind is None else kind
        src = own_ref.at[h] if (i, j) == (0, 0) else block(h, i, j, kind)
        c = pltpu.make_async_remote_copy(
            src_ref=src,
            dst_ref=block(h, *to, kind),
            send_sem=ss.at[h, number(h, *to), w],
            recv_sem=rs.at[h, number(h, *to), w],
            device_id=(neighbour(me, a, k), t),
            device_id_type=MESH,
        )
        c.start()
        sends.append(c)
        recvs[h, to[0] % SIDE, to[1] % SIDE, kind] = c

    def to_mate(h, i, j, kind=None):
        w = 0 if kind is None else kind
        src = own_ref.at[h] if (i, j) == (0, 0) else block(h, i, j, kind)
        c = pltpu.make_async_remote_copy(
            src_ref=src,
            dst_ref=block(h, i, j, kind),
            send_sem=ps.at[h, number(h, i, j), w],
            recv_sem=pr.at[h, number(h, i, j), w],
            device_id=(me, mate),
            device_id_type=MESH,
        )
        c.start()
        mates.setdefault(number(h, i, j), []).append(c)

    def got(h, i, j, kind=None):
        recvs[h, i, j, kind].wait_recv()

    both = (0, 1)
    local = []
    for h in both:
        c = pltpu.make_async_copy(own_ref.at[h], blocks[0].at[h, core], lsem.at[h])
        c.start()
        local.append(c)
    for h in both:
        for k in (1, 3):
            send(h, 0, 0, True, k)
    for h in both:
        to_mate(h, 0, 0)
        for k in (1, 3):
            send(h, 0, 0, False, k)

    def step_1():
        for h in both:
            for i, k, kind in ((3, 1, 0), (1, 3, 1)):
                got(h, i, 0)
                send(h, i, 0, True, k, kind)
                to_mate(h, i, 0)
        for h in both:
            for i in (3, 1):
                for k in (1, 3):
                    send(h, i, 0, False, k)

    def along_second(i):
        for h in both:
            for j, k, kind in ((3, 1, 0), (1, 3, 1)):
                got(h, i, j)
                send(h, i, j, False, k, kind)
                to_mate(h, i, j)

    def far_first():
        for h in both:
            for kind in (0, 1):
                got(h, 2, 0, kind)
                to_mate(h, 2, 0, kind)
            for k in (1, 3):
                send(h, 2, 0, False, k)

    def far_second(i):
        for h in both:
            for kind in (0, 1):
                got(h, i, 2, kind)
                to_mate(h, i, 2, kind)

    for r in range(16) if with_compute else ():
        rows = jnp.concatenate([q_ref[r, :, g * HD : (g + 1) * HD] for g in range(8)], axis=0)
        q_cols[r] = rows.T
    acc[...] = jnp.zeros_like(acc)
    acc_max[...] = jnp.full_like(acc_max, FLOOR_SCORE)
    v_cols[...] = jnp.ones_like(v_cols)

    def compute(dx, dz):
        n = dx * SIDE + dz
        if n == 0:
            for c in local:
                c.wait()
        for c in mates[n]:
            c.wait()
        if not with_compute:
            return
        ref = blocks[n]
        holder = lax.rem(place[0] + dx, SIDE) * SIDE + lax.rem(place[1] + dz, SIDE)
        for m in range(2):
            for half in range(2):
                v_cols[m, half * 64 : (half + 1) * 64, :] = ref[m, half, 1]
            k_rows[m] = jnp.concatenate([ref[m, 0, 0], ref[m, 1, 0]], axis=0).T

        def one_tile(i, _):
            request = tile_ref[holder * 12 + i]
            node = tile_ref[holder * 12 + 6 + i]
            score = jnp.dot(k_rows[node], q_cols[request], preferred_element_type=jnp.float32)
            top = jnp.max(score, axis=0, keepdims=True)
            weight = jnp.exp2(score * (SCALE * LOG2E) - top * (SCALE * LOG2E)).astype(jnp.bfloat16)
            mixed = jnp.dot(v_cols[node], weight, preferred_element_type=jnp.float32)
            part[i] = mixed[: HD + 8]
            part_max[i] = jnp.broadcast_to(top * SCALE, (8, 256))
            return 0

        lax.fori_loop(0, 6, one_tile, 0)

        def one_request(r, _):
            slot = slot_ref[holder * 32 + r]
            named = slot_ref[holder * 32 + 16 + r]
            here = named > 0
            new = jnp.where(here, part_max[slot], FLOOR_SCORE)
            old = acc_max[r]
            top = jnp.maximum(old, new)
            keep = jnp.exp(old - top)[:1]
            add = jnp.where(here, jnp.exp(new - top), 0.0)[:1]
            acc[r] = acc[r] * keep + part[slot] * add
            acc_max[r] = top
            return 0

        lax.fori_loop(0, 16, one_request, 0)

    step_1()
    compute(0, 0)
    along_second(0)
    compute(1, 0)
    far_first()
    compute(3, 0)
    compute(0, 1)
    along_second(3)
    along_second(1)
    compute(0, 3)
    far_second(0)
    compute(1, 1)
    along_second(2)
    compute(2, 0)
    compute(0, 2)
    far_second(3)
    far_second(1)
    far_second(2)
    for dx, dz in ((1, 3), (3, 1), (3, 3), (2, 1), (2, 3), (1, 2), (3, 2), (2, 2)):
        compute(dx, dz)
    for c in sends:
        c.wait_send()

    for r in range(16) if with_compute else ():
        total = acc[r, HD : HD + 1]
        some = total > 0.0
        inverse = jnp.where(some, 1.0 / jnp.where(some, total, 1.0), 0.0)
        rows = (acc[r, :HD] * inverse).T.astype(jnp.bfloat16)
        for g in range(8):
            o_ref[r, :, g * HD : (g + 1) * HD] = rows[g * 32 : (g + 1) * 32]
        level = acc_max[r, :1] + jnp.log(jnp.where(some, total, 1.0))
        lse_ref[r] = jnp.broadcast_to(jnp.where(some, level, FLOOR_SCORE), (8, 256))
    if not with_compute:
        o_ref[...] = q_ref[...]
        lse_ref[...] = jnp.zeros_like(lse_ref)


def run_tiles(tiles, slots, own, q, with_compute=True):
    vmem, smem = pl.BlockSpec(memory_space=pltpu.VMEM), pl.BlockSpec(memory_space=pltpu.SMEM)
    return pl.pallas_call(
        functools.partial(tiles_kernel, with_compute),
        out_shape=[jax.ShapeDtypeStruct((16, 32, 1024), jnp.bfloat16), jax.ShapeDtypeStruct((16, 8, 256), jnp.float32)],
        in_specs=[smem, smem, vmem, vmem],
        out_specs=[vmem, vmem],
        scratch_shapes=[
            *[pltpu.VMEM((2, 2, 2, 64, 1024), jnp.bfloat16) for _ in range(16)],
            pltpu.VMEM((16, HD, 256), jnp.bfloat16),
            pltpu.VMEM((2, 1024, HD), jnp.bfloat16),
            pltpu.VMEM((2, HD + 16, 1024), jnp.bfloat16),
            pltpu.VMEM((6, HD + 8, 256), jnp.float32),
            pltpu.VMEM((6, 8, 256), jnp.float32),
            pltpu.VMEM((16, HD + 8, 256), jnp.float32),
            pltpu.VMEM((16, 8, 256), jnp.float32),
            *[pltpu.SemaphoreType.DMA((2, 16, 2)) for _ in range(4)],
            pltpu.SemaphoreType.DMA((2,)),
        ],
        compiler_params=pltpu.CompilerParams(collective_id=3, has_side_effects=True, vmem_limit_bytes=48 * MIB),
    )(tiles, slots, own, q)


def merge_kernel(len_ref, q_ref, k_ref, v_ref, far_ref, lse_ref, o_ref):
    count = len_ref[0]
    rows = lax.broadcasted_iota(jnp.int32, (512, 512), 0)
    cols = lax.broadcasted_iota(jnp.int32, (512, 512), 1)
    allowed = (cols <= rows) & (cols < count)
    valid = rows[:, :1] < count
    for h in range(8):
        lanes = slice(h * HD, (h + 1) * HD)
        score = (
            lax.dot_general(q_ref[:, lanes], k_ref[...], (((1,), (1,)), ((), ())), preferred_element_type=jnp.float32) * SCALE
        )
        score = jnp.where(allowed, score, FLOOR_SCORE)
        top = jnp.max(score, axis=1, keepdims=True)
        weight = jnp.exp(score - top)
        total = jnp.sum(weight, axis=1, keepdims=True)
        mixed = jnp.dot(weight.astype(jnp.bfloat16), v_ref[...], preferred_element_type=jnp.float32)
        level = lse_ref[:, h : h + 1]
        peak = jnp.maximum(top, level)
        keep, add = jnp.exp(top - peak), jnp.exp(level - peak)
        far = far_ref[:, lanes].astype(jnp.float32)
        result = (mixed * keep + far * add) / (total * keep + add)
        o_ref[:, lanes] = jnp.where(valid, result, 0.0).astype(jnp.bfloat16)


def merge(count, q, k, v, far, level):
    vmem, smem = pl.BlockSpec(memory_space=pltpu.VMEM), pl.BlockSpec(memory_space=pltpu.SMEM)
    return pl.pallas_call(
        merge_kernel,
        out_shape=jax.ShapeDtypeStruct((512, 1024), jnp.bfloat16),
        in_specs=[smem] + [vmem] * 5,
        out_specs=vmem,
        compiler_params=pltpu.CompilerParams(vmem_limit_bytes=48 * MIB),
    )(count, q, k, v, far, level)


def body(queries, new_keys, new_values, key_cache, value_cache, page_owner, page_slot, tile_req, tile_node, suffix_len):
    dp_size = lax.axis_size("dp")
    dp_index = lax.axis_index("dp")
    parity = lax.axis_index("tensor") % 2
    owners = page_owner.reshape(dp_size, 16)
    slot_ids = page_slot.reshape(dp_size, 16)
    order = jnp.arange(16)
    same = owners[:, :, None] == owners[:, None, :]
    rank = jnp.sum(same & (order[None, :] < order[:, None])[None], axis=2)
    chosen = (owners[:, :, None] == dp_index) & (rank[:, :, None] == jnp.arange(CAP)[None, None, :])
    picked = jnp.sum(jnp.where(chosen, slot_ids[:, :, None], 0), axis=1)
    key_pages, value_pages = jnp.swapaxes(key_cache, 1, 2), jnp.swapaxes(value_cache, 1, 2)
    outgoing = jnp.stack([key_pages[picked], value_pages[picked]], axis=1)
    got = exchange(outgoing.reshape(4, 4, 512, 128), 0, 1).reshape(16, 2, CAP, 64, 128)
    my_owner = lax.dynamic_index_in_dim(owners, dp_index, 0, keepdims=False)
    my_rank = lax.dynamic_index_in_dim(rank, dp_index, 0, keepdims=False)
    rows = got[my_owner, :, my_rank].reshape(2, 8, 2, 64, 128)
    own = jnp.transpose(rows, (0, 2, 3, 1, 4)).reshape(2, 2, 64, 1024)

    spread = exchange(queries.reshape(4, 4, 32, 1024), 1, 2).reshape(16, 32, 1024)
    requests = tile_req.reshape(dp_size, 6)
    nodes = tile_node.reshape(dp_size, 6) - 2 * jnp.arange(dp_size, dtype=jnp.int32)[:, None]
    tiles = jnp.concatenate([requests, nodes], axis=1).reshape(-1)
    hits = requests[:, None, :] == jnp.arange(16)[None, :, None]
    slots = jnp.sum(jnp.where(hits, jnp.arange(6)[None, None, :], 0), axis=2)
    named = jnp.any(hits, axis=2)
    slots = jnp.concatenate([slots.astype(jnp.int32), named.astype(jnp.int32)], axis=1).reshape(-1)
    tile_out, tile_lse = run_tiles(tiles, slots, own, spread)

    far, level = exchange(tile_out.reshape(4, 4, 32, 1024), 1, 4, tile_lse)
    level = level[:, 0, :].reshape(16, 8, 32).transpose(0, 2, 1).reshape(512, 8)

    def join(block):
        other = from_partner(block)
        return jnp.concatenate([jnp.where(parity == 0, block, other), jnp.where(parity == 0, other, block)], axis=-1)

    keys, values = join(new_keys[0]), join(new_values[0])
    return merge(suffix_len, queries[0], keys, values, far.reshape(512, 1024), level)[None]


def solution(mesh):
    cut = P("dp", None, "tensor")
    return jax.shard_map(
        body,
        mesh=mesh,
        in_specs=(cut, cut, cut, cut, cut, P(), P(), P(), P(), P("dp")),
        out_specs=cut,
        check_vma=False,
    )
```

```python
import functools
import math

import jax
import jax.numpy as jnp
from jax import lax
from jax.experimental import pallas as pl
from jax.experimental.pallas import tpu as pltpu
from jax.sharding import PartitionSpec as P

HD = 128
CAP = 4
SIDE = 4
FLOOR_SCORE = -1e30
SCALE = 1.0 / math.sqrt(HD)
LOG2E = math.log2(math.e)
MESH = pl.DeviceIdType.MESH
MIB = 1 << 20


def from_partner(block):
    return lax.ppermute(block, "tensor", [(i, i ^ 1) for i in range(lax.axis_size("tensor"))])


def neighbour(me, axis, step):
    slow, fast = me // SIDE, me % SIDE
    if axis == 0:
        return lax.rem(slow + step, SIDE) * SIDE + fast
    return slow * SIDE + lax.rem(fast + step, SIDE)


def exchange_kernel(axis, with_small, *refs):
    if with_small:
        x_ref, y_ref, o_ref, oy_ref, mid, rel, s1, r1, s2, r2, lsem, ys, yr = refs
    else:
        x_ref, o_ref, mid, rel, s1, r1, s2, r2, lsem = refs
    me, t = lax.axis_index("dp"), lax.axis_index("tensor")
    place = (me // SIDE, me % SIDE)
    n = x_ref.shape[2 + axis] // 4

    def crd(a, k):
        return lax.rem(place[a] + k, SIDE)

    def cut(ref, start, size):
        return ref.at[:, start : start + size, :] if axis == 0 else ref.at[:, :, start : start + size]

    def quarter(ref, half, sub):
        return cut(ref, half * 2 * n, 2 * n) if sub is None else cut(ref, (half * 2 + sub) * n, n)

    def part(ref, sub):
        return ref if sub is None else cut(ref, sub * n, n)

    barrier = pltpu.get_barrier_semaphore()
    if with_small:
        for k in range(1, 16):
            pl.semaphore_signal(barrier, inc=1, device_id=(lax.rem(me + k, 16), t), device_id_type=MESH)
        pl.semaphore_wait(barrier, 15)
    else:
        for a in (0, 1):
            for k in (1, 3):
                pl.semaphore_signal(barrier, inc=1, device_id=(neighbour(me, a, k), t), device_id_type=MESH)
        pl.semaphore_wait(barrier, 4)

    def copy(src, dst, ss, rs, a, k):
        c = pltpu.make_async_remote_copy(
            src_ref=src, dst_ref=dst, send_sem=ss, recv_sem=rs, device_id=(neighbour(me, a, k), t), device_id_type=MESH
        )
        c.start()
        return c

    def phase(source, target, ss, rs, swap, relay):
        far, near = [], []
        for h in (0, 1):
            a = 1 - h if swap else h
            for j, k in ((0, 1), (1, 3)):
                far.append((h, j, k, copy(source(h, crd(a, 2), j), relay.at[h, j], ss.at[h, 0, j], rs.at[h, 0, j], a, k)))
            for j, k in ((0, 1), (1, 3)):
                near.append(copy(source(h, crd(a, k), None), target(h, crd(a, 0), None), ss.at[h, 1, j], rs.at[h, 1, j], a, k))
        for h, j, k, c in far:
            a = 1 - h if swap else h
            c.wait_recv()
            near.append(copy(relay.at[h, j], target(h, crd(a, 4 - k), j), ss.at[h, 2, j], rs.at[h, 2, j], a, k))
        for _, _, _, c in far:
            c.wait_send()
        return near

    def slab(ref, h, i):
        return ref.at[i] if h == 0 else ref.at[:, i]

    small = []
    if with_small:
        for k in range(1, 16):
            d = lax.rem(me + k, 16)
            c = pltpu.make_async_remote_copy(
                src_ref=y_ref.at[d], dst_ref=oy_ref.at[me], send_sem=ys.at[k], recv_sem=yr.at[k], device_id=(d, t), device_id_type=MESH
            )
            c.start()
            small.append(c)
        c = pltpu.make_async_copy(y_ref.at[me], oy_ref.at[me], ys.at[0])
        c.start()
        small.append(c)
    own = []
    for h in (0, 1):
        c = pltpu.make_async_copy(quarter(slab(x_ref, h, crd(h, 0)), h, None), mid.at[h, crd(h, 0)], lsem.at[h])
        c.start()
        own.append(c)
    flying = phase(
        lambda h, i, sub: quarter(slab(x_ref, h, i), h, sub), lambda h, i, sub: part(mid.at[h, i], sub), s1, r1, False, rel.at[0]
    )
    for c in own + flying:
        c.wait()

    def landing(h, b, sub):
        return quarter(o_ref.at[:, b] if h == 0 else o_ref.at[b], h, sub)

    own = []
    for h in (0, 1):
        b = crd(1 - h, 0)
        c = pltpu.make_async_copy(mid.at[h, :, b], landing(h, b, None), lsem.at[2 + h])
        c.start()
        own.append(c)
    flying = phase(lambda h, i, sub: part(mid.at[h, :, i], sub), landing, s2, r2, True, rel.at[1])
    for c in own + flying + small:
        c.wait()


def exchange(x, axis, collective_id, small=None):
    rows, lanes = x.shape[2:]
    half = (rows // 2, lanes) if axis == 0 else (rows, lanes // 2)
    sub = (rows // 4, lanes) if axis == 0 else (rows, lanes // 4)
    anywhere = pl.BlockSpec(memory_space=pl.ANY)
    args = (x,) if small is None else (x, small)
    scratch = [
        pltpu.VMEM((2, SIDE, SIDE) + half, x.dtype),
        pltpu.VMEM((2, 2, 2, SIDE) + sub, x.dtype),
        *[pltpu.SemaphoreType.DMA((2, 3, 2)) for _ in range(4)],
        pltpu.SemaphoreType.DMA((4,)),
    ]
    if small is not None:
        scratch += [pltpu.SemaphoreType.DMA((16,)), pltpu.SemaphoreType.DMA((16,))]
    out = pl.pallas_call(
        functools.partial(exchange_kernel, axis, small is not None),
        out_shape=[jax.ShapeDtypeStruct(a.shape, a.dtype) for a in args],
        in_specs=[anywhere] * len(args),
        out_specs=[anywhere] * len(args),
        scratch_shapes=scratch,
        compiler_params=pltpu.CompilerParams(collective_id=collective_id, has_side_effects=True, vmem_limit_bytes=32 * MIB),
    )(*args)
    return out[0] if small is None else out


ORDER = (
    (0, 0), (1, 0), (3, 0), (0, 1), (0, 3), (2, 0), (0, 2), (1, 1),
    (1, 3), (3, 1), (3, 3), (2, 1), (2, 3), (1, 2), (3, 2), (2, 2),
)


def pick(index, values):
    out = jnp.int32(values[0])
    for i, v in enumerate(values[1:], 1):
        out = jnp.where(index == i, jnp.int32(v), out)
    return out


def tiles_kernel(tile_ref, slot_ref, own_ref, q_ref, o_ref, lse_ref, *scratch):
    blocks, q_cols, k_rows, v_cols, part, part_max, acc, acc_max, ss, rs, ps, pr, lsem = scratch
    me, t = lax.axis_index("dp"), lax.axis_index("tensor")
    core = lax.rem(t, 2)
    mate = t + 1 - 2 * core
    place = (me // SIDE, me % SIDE)
    beside = {(a, k): neighbour(me, a, k) for a in (0, 1) for k in (1, 3)}

    barrier = pltpu.get_barrier_semaphore()
    for a in (0, 1):
        for k in (1, 3):
            pl.semaphore_signal(barrier, inc=1, device_id=(beside[a, k], t), device_id_type=MESH)
    pl.semaphore_signal(barrier, inc=1, device_id=(me, mate), device_id_type=MESH)
    pl.semaphore_wait(barrier, 5)

    def number(h, i, j):
        i, j = i % SIDE, j % SIDE
        return i * SIDE + j if h == 0 else j * SIDE + i

    def block(h, i, j, kind):
        ref = blocks.at[number(h, i, j), h, core]
        return ref if kind is None else ref.at[kind]

    def origin(h, i, j, kind):
        return own_ref.at[h] if (i, j) == (0, 0) else block(h, i, j, kind)

    def hop(h, i, j, first, k, kind, group):
        to = (i - k, j) if first else (i, j - k)
        pltpu.make_async_remote_copy(
            src_ref=origin(h, i, j, kind),
            dst_ref=block(h, *to, kind),
            send_sem=ss.at[0],
            recv_sem=rs.at[group],
            device_id=(beside[h if first else 1 - h, k], t),
            device_id_type=MESH,
        ).start()

    def taken(sem, holders_of_two):
        like = blocks.at[pl.ds(0, holders_of_two), :, 0]
        pltpu.make_async_copy(like, like, sem).wait()

    def across(n):
        return pltpu.make_async_remote_copy(
            src_ref=blocks.at[n, :, core],
            dst_ref=blocks.at[n, :, core],
            send_sem=ps.at[n],
            recv_sem=pr.at[n],
            device_id=(me, mate),
            device_id_type=MESH,
        )

    def to_mate(*holders_here):
        for dx, dz in holders_here:
            across(dx * SIDE + dz).start()

    both = (0, 1)
    local = []
    for h in both:
        c = pltpu.make_async_copy(own_ref.at[h], blocks.at[0, h, core], lsem.at[h])
        c.start()
        local.append(c)
    for h in both:
        for k in (1, 3):
            hop(h, 0, 0, True, k, None, 0)
    for h in both:
        for k in (1, 3):
            hop(h, 0, 0, False, k, None, 1)

    def near_first():
        taken(rs.at[0], 2)
        for h in both:
            hop(h, 3, 0, True, 1, 0, 2)
            hop(h, 1, 0, True, 3, 1, 2)

    def near_second(i, group):
        for h in both:
            hop(h, i, 3, False, 1, 0, group)
            hop(h, i, 1, False, 3, 1, group)

    def own_second():
        taken(rs.at[1], 2)
        near_second(0, 3)

    def near_on():
        for h in both:
            for i in (3, 1):
                for k in (1, 3):
                    hop(h, i, 0, False, k, None, 4)

    def far_first():
        taken(rs.at[2], 1)
        for h in both:
            for k in (1, 3):
                hop(h, 2, 0, False, k, None, 6)

    def far_own():
        taken(rs.at[3], 1)
        to_mate((2, 0), (0, 2))

    def near_near():
        taken(rs.at[4], 4)
        for i in (3, 1):
            near_second(i, 5)
        to_mate((1, 1), (1, 3), (3, 1), (3, 3))

    def far_near():
        taken(rs.at[6], 2)
        near_second(2, 7)

    def near_far():
        taken(rs.at[5], 2)
        to_mate((2, 1), (2, 3), (1, 2), (3, 2))

    def far_far():
        taken(rs.at[7], 1)
        to_mate((2, 2))

    def arrived(dx, dz):
        across(dx * SIDE + dz).wait()

    numbers = [dx * SIDE + dz for dx, dz in ORDER]
    holders = [lax.rem(place[0] + dx, SIDE) * SIDE + lax.rem(place[1] + dz, SIDE) for dx, dz in ORDER]

    def prepare(n, buf):
        for m in range(2):
            for half in range(2):
                v_cols[buf, m, half * 64 : (half + 1) * 64, :] = blocks[n, m, half, 1]
            k_rows[buf, m] = jnp.concatenate([blocks[n, m, 0, 0], blocks[n, m, 1, 0]], axis=0).T

    def compute(holder, buf):
        nodes = [tile_ref[holder * 12 + 6 + i] for i in range(6)]
        scores = [
            jnp.dot(k_rows[buf, nodes[i]], q_cols[tile_ref[holder * 12 + i]], preferred_element_type=jnp.float32)
            for i in range(6)
        ]
        for i in range(6):
            top = jnp.max(scores[i], axis=0, keepdims=True)
            weight = jnp.exp2(scores[i] * (SCALE * LOG2E) - top * (SCALE * LOG2E)).astype(jnp.bfloat16)
            mixed = jnp.dot(v_cols[buf, nodes[i]], weight, preferred_element_type=jnp.float32)
            part[buf, i] = mixed[: HD + 8]
            part_max[buf, i] = jnp.broadcast_to(top * SCALE, (8, 256))

    def combine(holder, buf):
        for r in range(16):
            slot = slot_ref[holder * 32 + r]
            here = slot_ref[holder * 32 + 16 + r] > 0
            new = jnp.where(here, part_max[buf, slot], FLOOR_SCORE)
            old = acc_max[r]
            top = jnp.maximum(old, new)
            keep = jnp.exp(old - top)[:1]
            add = jnp.where(here, jnp.exp(new - top), 0.0)[:1]
            acc[r] = acc[r] * keep + part[buf, slot] * add
            acc_max[r] = top

    for r in range(16):
        rows = jnp.concatenate([q_ref[r, :, g * HD : (g + 1) * HD] for g in range(8)], axis=0)
        q_cols[r] = rows.T
    acc[...] = jnp.zeros_like(acc)
    acc_max[...] = jnp.full_like(acc_max, FLOOR_SCORE)
    v_cols[...] = jnp.ones_like(v_cols)

    for c in local:
        c.wait()
    to_mate((0, 0))
    arrived(0, 0)
    prepare(0, 0)
    compute(holders[0], 0)
    near_first()
    own_second()
    near_on()
    to_mate((1, 0), (3, 0), (0, 1), (0, 3))
    arrived(*ORDER[1])
    prepare(numbers[1], 1)
    events = {1: far_first, 3: far_own, 5: near_near, 8: far_near, 9: near_far, 12: far_far}

    def step(at, _):
        for i in range(1, 15):

            @pl.when(at == i)
            def _(i=i):
                if i in events:
                    events[i]()
                arrived(*ORDER[i + 1])

        buf = at % 2
        combine(pick(at - 1, holders), 1 - buf)
        compute(pick(at, holders), buf)
        prepare(pick(at + 1, numbers + numbers[-1:]), 1 - buf)
        return 0

    lax.fori_loop(1, 16, step, 0)
    combine(holders[15], 1)
    taken(ss.at[0], 15)

    for r in range(16):
        total = acc[r, HD : HD + 1]
        some = total > 0.0
        inverse = jnp.where(some, 1.0 / jnp.where(some, total, 1.0), 0.0)
        rows = (acc[r, :HD] * inverse).T.astype(jnp.bfloat16)
        for g in range(8):
            o_ref[r, :, g * HD : (g + 1) * HD] = rows[g * 32 : (g + 1) * 32]
        level = acc_max[r, :1] + jnp.log(jnp.where(some, total, 1.0))
        lse_ref[r] = jnp.broadcast_to(jnp.where(some, level, FLOOR_SCORE), (8, 256))


def run_tiles(tiles, slots, own, q):
    vmem, smem = pl.BlockSpec(memory_space=pltpu.VMEM), pl.BlockSpec(memory_space=pltpu.SMEM)
    return pl.pallas_call(
        tiles_kernel,
        out_shape=[jax.ShapeDtypeStruct((16, 32, 1024), jnp.bfloat16), jax.ShapeDtypeStruct((16, 8, 256), jnp.float32)],
        in_specs=[smem, smem, vmem, vmem],
        out_specs=[vmem, vmem],
        scratch_shapes=[
            pltpu.VMEM((16, 2, 2, 2, 64, 1024), jnp.bfloat16),
            pltpu.VMEM((16, HD, 256), jnp.bfloat16),
            pltpu.VMEM((2, 2, 1024, HD), jnp.bfloat16),
            pltpu.VMEM((2, 2, HD + 16, 1024), jnp.bfloat16),
            pltpu.VMEM((2, 6, HD + 8, 256), jnp.float32),
            pltpu.VMEM((2, 6, 8, 256), jnp.float32),
            pltpu.VMEM((16, HD + 8, 256), jnp.float32),
            pltpu.VMEM((16, 8, 256), jnp.float32),
            pltpu.SemaphoreType.DMA((1,)),
            pltpu.SemaphoreType.DMA((8,)),
            pltpu.SemaphoreType.DMA((16,)),
            pltpu.SemaphoreType.DMA((16,)),
            pltpu.SemaphoreType.DMA((2,)),
        ],
        compiler_params=pltpu.CompilerParams(collective_id=3, has_side_effects=True, vmem_limit_bytes=48 * MIB),
    )(tiles, slots, own, q)


def merge_kernel(len_ref, q_ref, k_ref, v_ref, far_ref, lse_ref, o_ref):
    count = len_ref[0]
    rows = lax.broadcasted_iota(jnp.int32, (512, 512), 0)
    cols = lax.broadcasted_iota(jnp.int32, (512, 512), 1)
    allowed = (cols <= rows) & (cols < count)
    valid = rows[:, :1] < count
    for h in range(8):
        lanes = slice(h * HD, (h + 1) * HD)
        score = (
            lax.dot_general(q_ref[:, lanes], k_ref[...], (((1,), (1,)), ((), ())), preferred_element_type=jnp.float32) * SCALE
        )
        score = jnp.where(allowed, score, FLOOR_SCORE)
        top = jnp.max(score, axis=1, keepdims=True)
        weight = jnp.exp(score - top)
        total = jnp.sum(weight, axis=1, keepdims=True)
        mixed = jnp.dot(weight.astype(jnp.bfloat16), v_ref[...], preferred_element_type=jnp.float32)
        level = lse_ref[:, h : h + 1]
        peak = jnp.maximum(top, level)
        keep, add = jnp.exp(top - peak), jnp.exp(level - peak)
        far = far_ref[:, lanes].astype(jnp.float32)
        result = (mixed * keep + far * add) / (total * keep + add)
        o_ref[:, lanes] = jnp.where(valid, result, 0.0).astype(jnp.bfloat16)


def merge(count, q, k, v, far, level):
    vmem, smem = pl.BlockSpec(memory_space=pltpu.VMEM), pl.BlockSpec(memory_space=pltpu.SMEM)
    return pl.pallas_call(
        merge_kernel,
        out_shape=jax.ShapeDtypeStruct((512, 1024), jnp.bfloat16),
        in_specs=[smem] + [vmem] * 5,
        out_specs=vmem,
        compiler_params=pltpu.CompilerParams(vmem_limit_bytes=48 * MIB),
    )(count, q, k, v, far, level)


def body(queries, new_keys, new_values, key_cache, value_cache, page_owner, page_slot, tile_req, tile_node, suffix_len):
    dp_size = lax.axis_size("dp")
    dp_index = lax.axis_index("dp")
    parity = lax.axis_index("tensor") % 2
    owners = page_owner.reshape(dp_size, 16)
    slot_ids = page_slot.reshape(dp_size, 16)
    order = jnp.arange(16)
    same = owners[:, :, None] == owners[:, None, :]
    rank = jnp.sum(same & (order[None, :] < order[:, None])[None], axis=2)
    chosen = (owners[:, :, None] == dp_index) & (rank[:, :, None] == jnp.arange(CAP)[None, None, :])
    picked = jnp.sum(jnp.where(chosen, slot_ids[:, :, None], 0), axis=1)
    key_pages, value_pages = jnp.swapaxes(key_cache, 1, 2), jnp.swapaxes(value_cache, 1, 2)
    outgoing = jnp.stack([key_pages[picked], value_pages[picked]], axis=1)
    got = exchange(outgoing.reshape(4, 4, 512, 128), 0, 1).reshape(16, 2, CAP, 64, 128)
    my_owner = lax.dynamic_index_in_dim(owners, dp_index, 0, keepdims=False)
    my_rank = lax.dynamic_index_in_dim(rank, dp_index, 0, keepdims=False)
    rows = got[my_owner, :, my_rank].reshape(2, 8, 2, 64, 128)
    own = jnp.transpose(rows, (0, 2, 3, 1, 4)).reshape(2, 2, 64, 1024)

    spread = exchange(queries.reshape(4, 4, 32, 1024), 1, 2).reshape(16, 32, 1024)
    requests = tile_req.reshape(dp_size, 6)
    nodes = tile_node.reshape(dp_size, 6) - 2 * jnp.arange(dp_size, dtype=jnp.int32)[:, None]
    tiles = jnp.concatenate([requests, nodes], axis=1).reshape(-1)
    hits = requests[:, None, :] == jnp.arange(16)[None, :, None]
    slots = jnp.sum(jnp.where(hits, jnp.arange(6)[None, None, :], 0), axis=2)
    named = jnp.any(hits, axis=2)
    slots = jnp.concatenate([slots.astype(jnp.int32), named.astype(jnp.int32)], axis=1).reshape(-1)
    tile_out, tile_lse = run_tiles(tiles, slots, own, spread)

    far, level = exchange(tile_out.reshape(4, 4, 32, 1024), 1, 4, tile_lse)
    level = level[:, 0, :].reshape(16, 8, 32).transpose(0, 2, 1).reshape(512, 8)

    def join(block):
        other = from_partner(block)
        return jnp.concatenate([jnp.where(parity == 0, block, other), jnp.where(parity == 0, other, block)], axis=-1)

    keys, values = join(new_keys[0]), join(new_values[0])
    return merge(suffix_len, queries[0], keys, values, far.reshape(512, 1024), level)[None]


def solution(mesh):
    cut = P("dp", None, "tensor")
    return jax.shard_map(
        body,
        mesh=mesh,
        in_specs=(cut, cut, cut, cut, cut, P(), P(), P(), P(), P("dp")),
        out_specs=cut,
        check_vma=False,
    )
```

```python
import functools
import math

import jax
import jax.numpy as jnp
from jax import lax
from jax.experimental import pallas as pl
from jax.experimental.pallas import tpu as pltpu
from jax.sharding import PartitionSpec as P

HD = 128
CAP = 4
SIDE = 4
FLOOR_SCORE = -1e30
SCALE = 1.0 / math.sqrt(HD)
LOG2E = math.log2(math.e)
MESH = pl.DeviceIdType.MESH
MIB = 1 << 20


def neighbour(me, axis, step):
    slow, fast = me // SIDE, me % SIDE
    if axis == 0:
        return lax.rem(slow + step, SIDE) * SIDE + fast
    return slow * SIDE + lax.rem(fast + step, SIDE)


class Exchange:
    def __init__(self, me, tensor, x, out, mid, relay, sems, quarter, part):
        self.me, self.t, self.x, self.out, self.mid, self.relay = me, tensor, x, out, mid, relay
        self.s1, self.r1, self.s2, self.r2, self.local = sems
        self.place = (me // SIDE, me % SIDE)
        self.quarter, self.part = quarter, part

    def crd(self, a, k):
        return lax.rem(self.place[a] + k, SIDE)

    def copy(self, src, dst, ss, rs, a, k):
        c = pltpu.make_async_remote_copy(
            src_ref=src, dst_ref=dst, send_sem=ss, recv_sem=rs, device_id=(neighbour(self.me, a, k), self.t), device_id_type=MESH
        )
        c.start()
        return c

    def source(self, second, h, i, sub):
        if second:
            return self.part(self.mid.at[h, :, i], sub)
        return self.quarter(self.x.at[i] if h == 0 else self.x.at[:, i], h, sub)

    def target(self, second, h, i, sub):
        if second:
            return self.quarter(self.out.at[:, i] if h == 0 else self.out.at[i], h, sub)
        return self.part(self.mid.at[h, i], sub)

    def start(self, second):
        ss, rs = (self.s2, self.r2) if second else (self.s1, self.r1)
        self.far, self.near = [], []
        for h in (0, 1):
            a = 1 - h if second else h
            mine = self.crd(a, 0)
            for j, k in ((0, 1), (1, 3)):
                c = self.copy(
                    self.source(second, h, self.crd(a, 2), j), self.relay.at[int(second), h, j], ss.at[h, 0, j], rs.at[h, 0, j], a, k
                )
                self.far.append((h, j, k, a, c))
            for j, k in ((0, 1), (1, 3)):
                self.near.append(
                    self.copy(
                        self.source(second, h, self.crd(a, k), None), self.target(second, h, mine, None), ss.at[h, 1, j], rs.at[h, 1, j], a, k
                    )
                )
            c = pltpu.make_async_copy(self.source(second, h, mine, None), self.target(second, h, mine, None), self.local.at[int(second), h])
            c.start()
            self.near.append(c)

    def pass_on(self, second):
        ss, rs = (self.s2, self.r2) if second else (self.s1, self.r1)
        for h, j, k, a, c in self.far:
            c.wait_recv()
            to = self.target(second, h, self.crd(a, SIDE - k), j)
            self.near.append(self.copy(self.relay.at[int(second), h, j], to, ss.at[h, 2, j], rs.at[h, 2, j], a, k))

    def finish(self):
        for c in self.near:
            c.wait()
        for *_, c in self.far:
            c.wait_send()


def lanes_quarter(ref, half, sub):
    return ref.at[:, :, half * 512 : half * 512 + 512] if sub is None else lanes_part(ref, half * 2 + sub)


def lanes_part(ref, sub):
    return ref if sub is None else ref.at[:, :, sub * 256 : sub * 256 + 256]


def pages_quarter(ref, half, sub):
    return ref.at[:, half] if sub is None else ref.at[:, half, sub * 2 : sub * 2 + 2]


def pages_part(ref, sub):
    return ref if sub is None else ref.at[:, sub * 2 : sub * 2 + 2]


ORDER = (
    (0, 0), (1, 0), (3, 0), (0, 1), (0, 3), (2, 0), (0, 2), (1, 1),
    (1, 3), (3, 1), (3, 3), (2, 1), (2, 3), (1, 2), (3, 2), (2, 2),
)


def pick(index, values):
    out = jnp.int32(values[0])
    for i, v in enumerate(values[1:], 1):
        out = jnp.where(index == i, jnp.int32(v), out)
    return out


def attention_kernel(
    pick_ref, entry_ref, tile_ref, slot_ref, len_ref, key_ref, value_ref, q_ref, new_key_ref, new_value_ref, o_ref, *scratch
):
    page_out, page_in, page_mid, page_relay, q_in, q_mid, q_relay, far_in, far_mid, far_relay = scratch[:10]
    lse_out, lse_in, fresh, self_out, self_top, self_total, own_ref = scratch[10:17]
    blocks, q_cols, k_rows, v_cols, part, part_max, acc, acc_max, ss, rs, ps, pr, lsem = scratch[17:30]
    page_sems, q_sems, far_sems = scratch[30:35], scratch[35:40], scratch[40:45]
    small_send, small_recv, fresh_send, fresh_recv, fresh_local = scratch[45:]
    me, t = lax.axis_index("dp"), lax.axis_index("tensor")
    core = lax.rem(t, 2)
    mate = t + 1 - 2 * core
    place = (me // SIDE, me % SIDE)
    beside = {(a, k): neighbour(me, a, k) for a in (0, 1) for k in (1, 3)}
    both = (0, 1)

    barrier = pltpu.get_barrier_semaphore()
    for k in range(1, 16):
        pl.semaphore_signal(barrier, inc=1, device_id=(lax.rem(me + k, 16), t), device_id_type=MESH)
    pl.semaphore_signal(barrier, inc=1, device_id=(me, mate), device_id_type=MESH)
    for i in range(64):
        for kind, ref in enumerate((key_ref, value_ref)):
            page_out[i // 16, i // 4 % 4, kind, i % 4] = ref[pick_ref[i]]
    pl.semaphore_wait(barrier, 16)

    pages = Exchange(me, t, page_out, page_in, page_mid, page_relay, page_sems, pages_quarter, pages_part)
    spread = Exchange(me, t, q_ref, q_in, q_mid, q_relay, q_sems, lanes_quarter, lanes_part)
    pages.start(False)
    crossing = []
    for kind, ref in enumerate((new_key_ref, new_value_ref)):
        c = pltpu.make_async_remote_copy(
            src_ref=ref,
            dst_ref=fresh.at[core, kind],
            send_sem=fresh_send.at[kind],
            recv_sem=fresh_recv.at[kind],
            device_id=(me, mate),
            device_id_type=MESH,
        )
        c.start()
        crossing.append(c)
        c = pltpu.make_async_copy(ref, fresh.at[core, kind], fresh_local.at[kind])
        c.start()
        crossing.append(c)
    spread.start(False)
    for c in crossing:
        c.wait()

    count = len_ref[0]
    new_keys = jnp.concatenate([fresh[0, 0], fresh[1, 0]], axis=0)
    new_values = jnp.concatenate([fresh[0, 1], fresh[1, 1]], axis=0).T
    rows = lax.broadcasted_iota(jnp.int32, (512, 512), 0)
    cols = lax.broadcasted_iota(jnp.int32, (512, 512), 1)
    allowed = (cols <= rows) & (cols < count)

    def own_suffix(*heads):
        for h in heads:
            queries = q_ref[:, :, :, h * HD : (h + 1) * HD].reshape(512, HD)
            score = jnp.dot(queries, new_keys, preferred_element_type=jnp.float32) * SCALE
            score = jnp.where(allowed, score, FLOOR_SCORE)
            top = jnp.max(score, axis=1, keepdims=True)
            weight = jnp.exp(score - top)
            self_top[:, h : h + 1] = top
            self_total[:, h : h + 1] = jnp.sum(weight, axis=1, keepdims=True)
            self_out[h] = jnp.dot(weight.astype(jnp.bfloat16), new_values, preferred_element_type=jnp.float32)

    own_suffix(0, 1)
    pages.pass_on(False)
    own_suffix(2, 3)
    pages.finish()
    pages.start(True)
    spread.pass_on(False)
    own_suffix(4)
    spread.finish()
    spread.start(True)
    own_suffix(5)
    pages.pass_on(True)
    own_suffix(6, 7)
    pages.finish()
    for p in range(16):
        for kind in range(2):
            page = page_in[entry_ref[p], entry_ref[16 + p], kind, entry_ref[32 + p]]
            own_ref[p // 8, kind, :, p % 8 * 128 : p % 8 * 128 + 128] = page

    def number(h, i, j):
        i, j = i % SIDE, j % SIDE
        return i * SIDE + j if h == 0 else j * SIDE + i

    def block(h, i, j, kind):
        ref = blocks.at[number(h, i, j), h, core]
        return ref if kind is None else ref.at[kind]

    def origin(h, i, j, kind):
        return own_ref.at[h] if (i, j) == (0, 0) else block(h, i, j, kind)

    def hop(h, i, j, first, k, kind, group):
        to = (i - k, j) if first else (i, j - k)
        pltpu.make_async_remote_copy(
            src_ref=origin(h, i, j, kind),
            dst_ref=block(h, *to, kind),
            send_sem=ss.at[0],
            recv_sem=rs.at[group],
            device_id=(beside[h if first else 1 - h, k], t),
            device_id_type=MESH,
        ).start()

    def taken(sem, holders_of_two):
        like = blocks.at[pl.ds(0, holders_of_two), :, 0]
        pltpu.make_async_copy(like, like, sem).wait()

    def across(n):
        return pltpu.make_async_remote_copy(
            src_ref=blocks.at[n, :, core],
            dst_ref=blocks.at[n, :, core],
            send_sem=ps.at[n],
            recv_sem=pr.at[n],
            device_id=(me, mate),
            device_id_type=MESH,
        )

    def to_mate(*holders_here):
        for dx, dz in holders_here:
            across(dx * SIDE + dz).start()

    local = []
    for h in both:
        c = pltpu.make_async_copy(own_ref.at[h], blocks.at[0, h, core], lsem.at[h])
        c.start()
        local.append(c)
    for h in both:
        for k in (1, 3):
            hop(h, 0, 0, True, k, None, 0)
    for h in both:
        for k in (1, 3):
            hop(h, 0, 0, False, k, None, 1)

    def near_first():
        taken(rs.at[0], 2)
        for h in both:
            hop(h, 3, 0, True, 1, 0, 2)
            hop(h, 1, 0, True, 3, 1, 2)

    def near_second(i, group):
        for h in both:
            hop(h, i, 3, False, 1, 0, group)
            hop(h, i, 1, False, 3, 1, group)

    def own_second():
        taken(rs.at[1], 2)
        near_second(0, 3)

    def near_on():
        for h in both:
            for i in (3, 1):
                for k in (1, 3):
                    hop(h, i, 0, False, k, None, 4)

    def far_first():
        taken(rs.at[2], 1)
        for h in both:
            for k in (1, 3):
                hop(h, 2, 0, False, k, None, 6)

    def far_own():
        taken(rs.at[3], 1)
        to_mate((2, 0), (0, 2))

    def near_near():
        taken(rs.at[4], 4)
        for i in (3, 1):
            near_second(i, 5)
        to_mate((1, 1), (1, 3), (3, 1), (3, 3))

    def far_near():
        taken(rs.at[6], 2)
        near_second(2, 7)

    def near_far():
        taken(rs.at[5], 2)
        to_mate((2, 1), (2, 3), (1, 2), (3, 2))

    def far_far():
        taken(rs.at[7], 1)
        to_mate((2, 2))

    def arrived(dx, dz):
        across(dx * SIDE + dz).wait()

    numbers = [dx * SIDE + dz for dx, dz in ORDER]
    holders = [lax.rem(place[0] + dx, SIDE) * SIDE + lax.rem(place[1] + dz, SIDE) for dx, dz in ORDER]

    def prepare(n, buf):
        for m in range(2):
            for half in range(2):
                v_cols[buf, m, half * 64 : (half + 1) * 64, :] = blocks[n, m, half, 1]
            k_rows[buf, m] = jnp.concatenate([blocks[n, m, 0, 0], blocks[n, m, 1, 0]], axis=0).T

    def compute(holder, buf):
        nodes = [tile_ref[holder * 12 + 6 + i] for i in range(6)]

        def score_of(i):
            return jnp.dot(k_rows[buf, nodes[i]], q_cols[tile_ref[holder * 12 + i]], preferred_element_type=jnp.float32)

        scores = [score_of(i) for i in range(4)]
        for i in range(6):
            top = jnp.max(scores[i], axis=0, keepdims=True)
            weight = jnp.exp2(scores[i] * (SCALE * LOG2E) - top * (SCALE * LOG2E)).astype(jnp.bfloat16)
            if len(scores) < 6:
                scores.append(score_of(len(scores)))
            mixed = jnp.dot(v_cols[buf, nodes[i]], weight, preferred_element_type=jnp.float32)
            part[buf, i] = mixed[: HD + 8]
            part_max[buf, i] = jnp.broadcast_to(top * SCALE, (8, 256))

    def combine(holder, buf):
        for r in range(16):
            slot = slot_ref[holder * 32 + r]
            here = slot_ref[holder * 32 + 16 + r] > 0
            new = jnp.where(here, part_max[buf, slot], FLOOR_SCORE)
            old = acc_max[r]
            top = jnp.maximum(old, new)
            keep = jnp.exp(old - top)[:1]
            add = jnp.where(here, jnp.exp(new - top), 0.0)[:1]
            acc[r] = acc[r] * keep + part[buf, slot] * add
            acc_max[r] = top

    for c in local:
        c.wait()
    to_mate((0, 0))
    v_cols[...] = jnp.ones_like(v_cols)
    arrived(0, 0)
    prepare(0, 0)
    spread.pass_on(True)
    near_first()
    own_second()
    near_on()
    to_mate((1, 0), (3, 0), (0, 1), (0, 3))
    spread.finish()
    for r in range(16):
        rows = jnp.concatenate([q_in[r // SIDE, r % SIDE, :, g * HD : (g + 1) * HD] for g in range(8)], axis=0)
        q_cols[r] = rows.T
    acc[...] = jnp.zeros_like(acc)
    acc_max[...] = jnp.full_like(acc_max, FLOOR_SCORE)

    compute(holders[0], 0)
    arrived(*ORDER[1])
    prepare(numbers[1], 1)
    events = {1: far_first, 3: far_own, 5: near_near, 8: far_near, 9: near_far, 12: far_far}

    def step(at, _):
        for i in range(1, 15):

            @pl.when(at == i)
            def _(i=i):
                if i in events:
                    events[i]()
                arrived(*ORDER[i + 1])

        buf = at % 2
        combine(pick(at - 1, holders), 1 - buf)
        compute(pick(at, holders), buf)
        prepare(pick(at + 1, numbers + numbers[-1:]), 1 - buf)
        return 0

    lax.fori_loop(1, 16, step, 0)
    combine(holders[15], 1)
    taken(ss.at[0], 15)

    for r in range(16):
        total = acc[r, HD : HD + 1]
        some = total > 0.0
        inverse = jnp.where(some, 1.0 / jnp.where(some, total, 1.0), 0.0)
        rows = (acc[r, :HD] * inverse).T.astype(jnp.bfloat16)
        for g in range(8):
            q_in[r // SIDE, r % SIDE, :, g * HD : (g + 1) * HD] = rows[g * 32 : (g + 1) * 32]
        level = acc_max[r, :1] + jnp.log(jnp.where(some, total, 1.0))
        lse_out[r] = jnp.broadcast_to(jnp.where(some, level, FLOOR_SCORE), (8, 256))

    level_copies = []
    for k in range(1, 16):
        d = lax.rem(me + k, 16)
        c = pltpu.make_async_remote_copy(
            src_ref=lse_out.at[d],
            dst_ref=lse_in.at[me],
            send_sem=small_send.at[k],
            recv_sem=small_recv.at[k],
            device_id=(d, t),
            device_id_type=MESH,
        )
        c.start()
        level_copies.append(c)
    c = pltpu.make_async_copy(lse_out.at[me], lse_in.at[me], small_send.at[0])
    c.start()
    level_copies.append(c)
    back = Exchange(me, t, q_in, far_in, far_mid, far_relay, far_sems, lanes_quarter, lanes_part)
    for second in (False, True):
        back.start(second)
        back.pass_on(second)
        back.finish()
    for c in level_copies:
        c.wait()

    def merge(holder, _):
        here = pl.ds(pl.multiple_of(holder * 32, 32), 32)
        levels = lse_in[holder].T[:, :1]
        tops, totals = self_top[here, :], self_total[here, :]
        valid = lax.broadcasted_iota(jnp.int32, (32, HD), 0) + holder * 32 < count
        for h in range(8):
            lanes = slice(h * HD, (h + 1) * HD)
            top, total = tops[:, h : h + 1], totals[:, h : h + 1]
            level = levels[h * 32 : (h + 1) * 32]
            peak = jnp.maximum(top, level)
            keep, add = jnp.exp(top - peak), jnp.exp(level - peak)
            inverse = 1.0 / (total * keep + add)
            far = far_in[holder // SIDE, holder % SIDE, :, lanes].astype(jnp.float32)
            result = self_out[h, here] * (keep * inverse) + far * (add * inverse)
            o_ref[here, lanes] = jnp.where(valid, result, 0.0).astype(jnp.bfloat16)
        return 0

    lax.fori_loop(0, 16, merge, 0)


def attend(tables, arrays):
    vmem, smem = pl.BlockSpec(memory_space=pltpu.VMEM), pl.BlockSpec(memory_space=pltpu.SMEM)
    dma, bf16, f32 = pltpu.SemaphoreType.DMA, jnp.bfloat16, jnp.float32
    flat = (SIDE, SIDE, 32, 1024)
    exchange_sems = [dma((2, 3, 2))] * 4 + [dma((2, 2))]
    return pl.pallas_call(
        attention_kernel,
        out_shape=jax.ShapeDtypeStruct((512, 1024), bf16),
        in_specs=[smem] * len(tables) + [vmem] * len(arrays),
        out_specs=vmem,
        scratch_shapes=[
            pltpu.VMEM((SIDE, SIDE, 2, CAP, 64, 128), bf16),
            pltpu.VMEM((SIDE, SIDE, 2, CAP, 64, 128), bf16),
            pltpu.VMEM((2, SIDE, SIDE, CAP, 64, 128), bf16),
            pltpu.VMEM((2, 2, 2, SIDE, 2, 64, 128), bf16),
            pltpu.VMEM(flat, bf16),
            pltpu.VMEM((2, SIDE, SIDE, 32, 512), bf16),
            pltpu.VMEM((2, 2, 2, SIDE, 32, 256), bf16),
            pltpu.VMEM(flat, bf16),
            pltpu.VMEM((2, SIDE, SIDE, 32, 512), bf16),
            pltpu.VMEM((2, 2, 2, SIDE, 32, 256), bf16),
            pltpu.VMEM((16, 8, 256), f32),
            pltpu.VMEM((16, 8, 256), f32),
            pltpu.VMEM((2, 2, 64, 512), bf16),
            pltpu.VMEM((8, 512, HD), f32),
            pltpu.VMEM((512, HD), f32),
            pltpu.VMEM((512, HD), f32),
            pltpu.VMEM((2, 2, 64, 1024), bf16),
            pltpu.VMEM((16, 2, 2, 2, 64, 1024), bf16),
            pltpu.VMEM((16, HD, 256), bf16),
            pltpu.VMEM((2, 2, 1024, HD), bf16),
            pltpu.VMEM((2, 2, HD + 16, 1024), bf16),
            pltpu.VMEM((2, 6, HD + 8, 256), f32),
            pltpu.VMEM((2, 6, 8, 256), f32),
            pltpu.VMEM((16, HD + 8, 256), f32),
            pltpu.VMEM((16, 8, 256), f32),
            dma((1,)),
            dma((8,)),
            dma((16,)),
            dma((16,)),
            dma((2,)),
            *exchange_sems,
            *exchange_sems,
            *exchange_sems,
            dma((16,)),
            dma((16,)),
            dma((2,)),
            dma((2,)),
            dma((2,)),
        ],
        compiler_params=pltpu.CompilerParams(collective_id=1, has_side_effects=True, vmem_limit_bytes=50 * MIB),
    )(*tables, *arrays)


def body(queries, new_keys, new_values, key_cache, value_cache, page_owner, page_slot, tile_req, tile_node, suffix_len):
    dp_size = lax.axis_size("dp")
    dp_index = lax.axis_index("dp")
    owners = page_owner.reshape(dp_size, 16)
    slot_ids = page_slot.reshape(dp_size, 16)
    order = jnp.arange(16)
    same = owners[:, :, None] == owners[:, None, :]
    rank = jnp.sum(same & (order[None, :] < order[:, None])[None], axis=2, dtype=jnp.int32)
    chosen = (owners[:, :, None] == dp_index) & (rank[:, :, None] == jnp.arange(CAP)[None, None, :])
    picked = jnp.sum(jnp.where(chosen, slot_ids[:, :, None], 0), axis=1, dtype=jnp.int32).reshape(-1)
    my_owner = lax.dynamic_index_in_dim(owners, dp_index, 0, keepdims=False)
    my_rank = lax.dynamic_index_in_dim(rank, dp_index, 0, keepdims=False)
    entries = jnp.concatenate([my_owner // SIDE, my_owner % SIDE, my_rank])
    requests = tile_req.reshape(dp_size, 6)
    nodes = tile_node.reshape(dp_size, 6) - 2 * jnp.arange(dp_size, dtype=jnp.int32)[:, None]
    tiles = jnp.concatenate([requests, nodes], axis=1).reshape(-1)
    hits = requests[:, None, :] == jnp.arange(16)[None, :, None]
    slots = jnp.sum(jnp.where(hits, jnp.arange(6)[None, None, :], 0), axis=2)
    named = jnp.any(hits, axis=2)
    slots = jnp.concatenate([slots.astype(jnp.int32), named.astype(jnp.int32)], axis=1).reshape(-1)
    arrays = (
        jnp.swapaxes(key_cache, 1, 2),
        jnp.swapaxes(value_cache, 1, 2),
        queries.reshape(SIDE, SIDE, 32, 1024),
        new_keys[0].T,
        new_values[0].T,
    )
    return attend((picked, entries, tiles, slots, suffix_len), arrays)[None]


def solution(mesh):
    cut = P("dp", None, "tensor")
    return jax.shard_map(
        body,
        mesh=mesh,
        in_specs=(cut, cut, cut, cut, cut, P(), P(), P(), P(), P("dp")),
        out_specs=cut,
        check_vma=False,
    )
```

```python
import functools
import math

import jax
import jax.numpy as jnp
from jax import lax
from jax.experimental import pallas as pl
from jax.experimental.pallas import tpu as pltpu
from jax.sharding import PartitionSpec as P

HD = 128
CAP = 4
SIDE = 4
FLOOR_SCORE = -1e30
SCALE = 1.0 / math.sqrt(HD)
LOG2E = math.log2(math.e)
MESH = pl.DeviceIdType.MESH
MIB = 1 << 20


def neighbour(me, axis, step):
    slow, fast = me // SIDE, me % SIDE
    if axis == 0:
        return lax.rem(slow + step, SIDE) * SIDE + fast
    return slow * SIDE + lax.rem(fast + step, SIDE)


class Exchange:
    def __init__(self, me, tensor, x, out, mid, relay, sems, quarter, part):
        self.me, self.t, self.x, self.out, self.mid, self.relay = me, tensor, x, out, mid, relay
        self.s1, self.r1, self.s2, self.r2, self.local = sems
        self.place = (me // SIDE, me % SIDE)
        self.quarter, self.part = quarter, part

    def crd(self, a, k):
        return lax.rem(self.place[a] + k, SIDE)

    def copy(self, src, dst, ss, rs, a, k):
        c = pltpu.make_async_remote_copy(
            src_ref=src, dst_ref=dst, send_sem=ss, recv_sem=rs, device_id=(neighbour(self.me, a, k), self.t), device_id_type=MESH
        )
        c.start()
        return c

    def source(self, second, h, i, sub):
        if second:
            return self.part(self.mid.at[h, :, i], sub)
        return self.quarter(self.x.at[i] if h == 0 else self.x.at[:, i], h, sub)

    def target(self, second, h, i, sub):
        if second:
            return self.quarter(self.out.at[:, i] if h == 0 else self.out.at[i], h, sub)
        return self.part(self.mid.at[h, i], sub)

    def start(self, second):
        ss, rs = (self.s2, self.r2) if second else (self.s1, self.r1)
        self.far, self.near = [], []
        for h in (0, 1):
            a = 1 - h if second else h
            mine = self.crd(a, 0)
            for j, k in ((0, 1), (1, 3)):
                c = self.copy(
                    self.source(second, h, self.crd(a, 2), j), self.relay.at[int(second), h, j], ss.at[h, 0, j], rs.at[h, 0, j], a, k
                )
                self.far.append((h, j, k, a, c))
            for j, k in ((0, 1), (1, 3)):
                self.near.append(
                    self.copy(
                        self.source(second, h, self.crd(a, k), None), self.target(second, h, mine, None), ss.at[h, 1, j], rs.at[h, 1, j], a, k
                    )
                )
            c = pltpu.make_async_copy(self.source(second, h, mine, None), self.target(second, h, mine, None), self.local.at[int(second), h])
            c.start()
            self.near.append(c)

    def pass_on(self, second):
        ss, rs = (self.s2, self.r2) if second else (self.s1, self.r1)
        for h, j, k, a, c in self.far:
            c.wait_recv()
            to = self.target(second, h, self.crd(a, SIDE - k), j)
            self.near.append(self.copy(self.relay.at[int(second), h, j], to, ss.at[h, 2, j], rs.at[h, 2, j], a, k))

    def finish(self):
        for c in self.near:
            c.wait()
        for *_, c in self.far:
            c.wait_send()


def lanes_quarter(ref, half, sub):
    return ref.at[:, :, half * 512 : half * 512 + 512] if sub is None else lanes_part(ref, half * 2 + sub)


def lanes_part(ref, sub):
    return ref if sub is None else ref.at[:, :, sub * 256 : sub * 256 + 256]


def pages_quarter(ref, half, sub):
    return ref.at[:, half] if sub is None else ref.at[:, half, sub * 2 : sub * 2 + 2]


def pages_part(ref, sub):
    return ref if sub is None else ref.at[:, sub * 2 : sub * 2 + 2]


ORDER = (
    (0, 0), (1, 0), (3, 0), (0, 1), (0, 3), (2, 0), (0, 2), (1, 1),
    (1, 3), (3, 1), (3, 3), (2, 1), (2, 3), (1, 2), (3, 2), (2, 2),
)


def pick(index, values):
    out = jnp.int32(values[0])
    for i, v in enumerate(values[1:], 1):
        out = jnp.where(index == i, jnp.int32(v), out)
    return out


def attention_kernel(
    pick_ref, entry_ref, tile_ref, slot_ref, len_ref, key_ref, value_ref, q_ref, new_key_ref, new_value_ref, o_ref, *scratch
):
    page_out, page_in, page_mid, page_relay, q_in, q_mid, q_relay, far_in, far_mid, far_relay = scratch[:10]
    lse_out, lse_in, fresh, self_out, self_top, self_total, own_ref = scratch[10:17]
    blocks, q_cols, k_rows, v_cols, part, part_max, acc, acc_max, ss, rs, ps, pr, lsem = scratch[17:30]
    page_sems, q_sems, far_sems = scratch[30:35], scratch[35:40], scratch[40:45]
    small_send, small_recv, fresh_send, fresh_recv, fresh_local = scratch[45:]
    me, t = lax.axis_index("dp"), lax.axis_index("tensor")
    core = lax.rem(t, 2)
    mate = t + 1 - 2 * core
    place = (me // SIDE, me % SIDE)
    beside = {(a, k): neighbour(me, a, k) for a in (0, 1) for k in (1, 3)}
    both = (0, 1)

    barrier = pltpu.get_barrier_semaphore()
    for k in range(1, 16):
        pl.semaphore_signal(barrier, inc=1, device_id=(lax.rem(me + k, 16), t), device_id_type=MESH)
    pl.semaphore_signal(barrier, inc=1, device_id=(me, mate), device_id_type=MESH)
    for i in range(64):
        for kind, ref in enumerate((key_ref, value_ref)):
            page_out[i // 16, i // 4 % 4, kind, i % 4] = ref[pick_ref[i]]
    pl.semaphore_wait(barrier, 16)

    pages = Exchange(me, t, page_out, page_in, page_mid, page_relay, page_sems, pages_quarter, pages_part)
    spread = Exchange(me, t, q_ref, q_in, q_mid, q_relay, q_sems, lanes_quarter, lanes_part)
    pages.start(False)
    crossing = []
    for kind, ref in enumerate((new_key_ref, new_value_ref)):
        c = pltpu.make_async_remote_copy(
            src_ref=ref,
            dst_ref=fresh.at[core, kind],
            send_sem=fresh_send.at[kind],
            recv_sem=fresh_recv.at[kind],
            device_id=(me, mate),
            device_id_type=MESH,
        )
        c.start()
        crossing.append(c)
        c = pltpu.make_async_copy(ref, fresh.at[core, kind], fresh_local.at[kind])
        c.start()
        crossing.append(c)
    spread.start(False)
    for c in crossing:
        c.wait()

    count = len_ref[0]
    new_keys = jnp.concatenate([fresh[0, 0], fresh[1, 0]], axis=0)
    new_values = jnp.concatenate([fresh[0, 1], fresh[1, 1]], axis=0).T
    rows = lax.broadcasted_iota(jnp.int32, (512, 512), 0)
    cols = lax.broadcasted_iota(jnp.int32, (512, 512), 1)
    allowed = (cols <= rows) & (cols < count)

    def own_suffix(*heads):
        for h in heads:
            queries = q_ref[:, :, :, h * HD : (h + 1) * HD].reshape(512, HD)
            score = jnp.dot(queries, new_keys, preferred_element_type=jnp.float32) * SCALE
            score = jnp.where(allowed, score, FLOOR_SCORE)
            top = jnp.max(score, axis=1, keepdims=True)
            weight = jnp.exp(score - top)
            self_top[:, h : h + 1] = top
            self_total[:, h : h + 1] = jnp.sum(weight, axis=1, keepdims=True)
            self_out[h] = jnp.dot(weight.astype(jnp.bfloat16), new_values, preferred_element_type=jnp.float32)

    own_suffix(0, 1)
    pages.pass_on(False)
    own_suffix(2, 3)
    pages.finish()
    pages.start(True)
    spread.pass_on(False)
    own_suffix(4)
    spread.finish()
    spread.start(True)
    own_suffix(5)
    pages.pass_on(True)
    own_suffix(6, 7)
    pages.finish()
    for p in range(16):
        for kind in range(2):
            page = page_in[entry_ref[p], entry_ref[16 + p], kind, entry_ref[32 + p]]
            own_ref[p // 8, kind, :, p % 8 * 128 : p % 8 * 128 + 128] = page

    def number(h, i, j):
        i, j = i % SIDE, j % SIDE
        return i * SIDE + j if h == 0 else j * SIDE + i

    def block(h, i, j, kind):
        ref = blocks.at[number(h, i, j), h, core]
        return ref if kind is None else ref.at[kind]

    def origin(h, i, j, kind):
        return own_ref.at[h] if (i, j) == (0, 0) else block(h, i, j, kind)

    def hop(h, i, j, first, k, kind, group):
        to = (i - k, j) if first else (i, j - k)
        pltpu.make_async_remote_copy(
            src_ref=origin(h, i, j, kind),
            dst_ref=block(h, *to, kind),
            send_sem=ss.at[0],
            recv_sem=rs.at[group],
            device_id=(beside[h if first else 1 - h, k], t),
            device_id_type=MESH,
        ).start()

    def taken(sem, holders_of_two):
        like = blocks.at[pl.ds(0, holders_of_two), :, 0]
        pltpu.make_async_copy(like, like, sem).wait()

    def across(n):
        return pltpu.make_async_remote_copy(
            src_ref=blocks.at[n, :, core],
            dst_ref=blocks.at[n, :, core],
            send_sem=ps.at[n],
            recv_sem=pr.at[n],
            device_id=(me, mate),
            device_id_type=MESH,
        )

    def to_mate(*holders_here):
        for dx, dz in holders_here:
            across(dx * SIDE + dz).start()

    local = []
    for h in both:
        c = pltpu.make_async_copy(own_ref.at[h], blocks.at[0, h, core], lsem.at[h])
        c.start()
        local.append(c)
    for h in both:
        for k in (1, 3):
            hop(h, 0, 0, True, k, None, 0)
    for h in both:
        for k in (1, 3):
            hop(h, 0, 0, False, k, None, 1)

    def near_first():
        taken(rs.at[0], 2)
        for h in both:
            hop(h, 3, 0, True, 1, 0, 2)
            hop(h, 1, 0, True, 3, 1, 2)

    def near_second(i, group):
        for h in both:
            hop(h, i, 3, False, 1, 0, group)
            hop(h, i, 1, False, 3, 1, group)

    def own_second():
        taken(rs.at[1], 2)
        near_second(0, 3)

    def near_on():
        for h in both:
            for i in (3, 1):
                for k in (1, 3):
                    hop(h, i, 0, False, k, None, 4)

    def far_first():
        taken(rs.at[2], 1)
        for h in both:
            for k in (1, 3):
                hop(h, 2, 0, False, k, None, 6)

    def far_own():
        taken(rs.at[3], 1)
        to_mate((2, 0), (0, 2))

    def near_near():
        taken(rs.at[4], 4)
        for i in (3, 1):
            near_second(i, 5)
        to_mate((1, 1), (1, 3), (3, 1), (3, 3))

    def far_near():
        taken(rs.at[6], 2)
        near_second(2, 7)

    def near_far():
        taken(rs.at[5], 2)
        to_mate((2, 1), (2, 3), (1, 2), (3, 2))

    def far_far():
        taken(rs.at[7], 1)
        to_mate((2, 2))

    def arrived(dx, dz):
        across(dx * SIDE + dz).wait()

    numbers = [dx * SIDE + dz for dx, dz in ORDER]
    holders = [lax.rem(place[0] + dx, SIDE) * SIDE + lax.rem(place[1] + dz, SIDE) for dx, dz in ORDER]

    def prepare(n, buf):
        for m in range(2):
            for half in range(2):
                v_cols[buf, m, half * 64 : (half + 1) * 64, :] = blocks[n, m, half, 1]
            k_rows[buf, m] = jnp.concatenate([blocks[n, m, 0, 0], blocks[n, m, 1, 0]], axis=0).T

    def compute(holder, buf):
        nodes = [tile_ref[holder * 12 + 6 + i] for i in range(6)]

        def score_of(i):
            return jnp.dot(k_rows[buf, nodes[i]], q_cols[tile_ref[holder * 12 + i]], preferred_element_type=jnp.float32)

        scores = [score_of(i) for i in range(4)]
        for i in range(6):
            top = jnp.max(scores[i], axis=0, keepdims=True)
            weight = jnp.exp2(scores[i] * (SCALE * LOG2E) - top * (SCALE * LOG2E)).astype(jnp.bfloat16)
            if len(scores) < 6:
                scores.append(score_of(len(scores)))
            mixed = jnp.dot(v_cols[buf, nodes[i]], weight, preferred_element_type=jnp.float32)
            part[buf, i] = mixed[: HD + 8]
            part_max[buf, i] = jnp.broadcast_to(top * SCALE, (8, 256))

    def combine(holder, buf):
        for r in range(16):
            slot = slot_ref[holder * 32 + r]
            here = slot_ref[holder * 32 + 16 + r] > 0
            new = jnp.where(here, part_max[buf, slot], FLOOR_SCORE)
            old = acc_max[r]
            top = jnp.maximum(old, new)
            keep = jnp.exp(old - top)[:1]
            add = jnp.where(here, jnp.exp(new - top), 0.0)[:1]
            acc[r] = acc[r] * keep + part[buf, slot] * add
            acc_max[r] = top

    for c in local:
        c.wait()
    to_mate((0, 0))
    v_cols[...] = jnp.ones_like(v_cols)
    arrived(0, 0)
    prepare(0, 0)
    spread.pass_on(True)
    near_first()
    own_second()
    near_on()
    to_mate((1, 0), (3, 0), (0, 1), (0, 3))
    spread.finish()
    for r in range(16):
        rows = jnp.concatenate([q_in[r // SIDE, r % SIDE, :, g * HD : (g + 1) * HD] for g in range(8)], axis=0)
        q_cols[r] = rows.T
    acc[...] = jnp.zeros_like(acc)
    lse_out[...] = jnp.zeros_like(lse_out)
    acc_max[...] = jnp.full_like(acc_max, FLOOR_SCORE)

    compute(holders[0], 0)
    arrived(*ORDER[1])
    prepare(numbers[1], 1)
    events = {1: far_first, 3: far_own, 5: near_near, 8: far_near, 9: near_far, 12: far_far}

    def step(at, _):
        for i in range(1, 15):

            @pl.when(at == i)
            def _(i=i):
                if i in events:
                    events[i]()
                arrived(*ORDER[i + 1])

        buf = at % 2
        combine(pick(at - 1, holders), 1 - buf)
        compute(pick(at, holders), buf)
        prepare(pick(at + 1, numbers + numbers[-1:]), 1 - buf)
        return 0

    lax.fori_loop(1, 16, step, 0)
    combine(holders[15], 1)
    taken(ss.at[0], 15)

    for r in range(16):
        total = acc[r, HD : HD + 1]
        some = total > 0.0
        inverse = jnp.where(some, 1.0 / jnp.where(some, total, 1.0), 0.0)
        rows = (acc[r, :HD] * inverse).T.astype(jnp.bfloat16)
        for g in range(8):
            q_in[r // SIDE, r % SIDE, :, g * HD : (g + 1) * HD] = rows[g * 32 : (g + 1) * 32]
        level = acc_max[r, :1] + jnp.log(jnp.where(some, total, 1.0))
        level = jnp.where(some, level, FLOOR_SCORE)
        for g in range(8):
            lse_out[r, g : g + 1, :32] = level[:, g * 32 : (g + 1) * 32]

    level_copies = []
    for k in range(1, 16):
        d = lax.rem(me + k, 16)
        c = pltpu.make_async_remote_copy(
            src_ref=lse_out.at[d],
            dst_ref=lse_in.at[me],
            send_sem=small_send.at[k],
            recv_sem=small_recv.at[k],
            device_id=(d, t),
            device_id_type=MESH,
        )
        c.start()
        level_copies.append(c)
    c = pltpu.make_async_copy(lse_out.at[me], lse_in.at[me], small_send.at[0])
    c.start()
    level_copies.append(c)
    back = Exchange(me, t, q_in, far_in, far_mid, far_relay, far_sems, lanes_quarter, lanes_part)
    for second in (False, True):
        back.start(second)
        back.pass_on(second)
        back.finish()
    for c in level_copies:
        c.wait()

    def merge(holder, _):
        here = pl.ds(pl.multiple_of(holder * 32, 32), 32)
        levels = lse_in[holder].T[:32, :8]
        tops, totals = self_top[here, :8], self_total[here, :8]
        peak = jnp.maximum(tops, levels)
        keep, add = jnp.exp(tops - peak), jnp.exp(levels - peak)
        inverse = 1.0 / (totals * keep + add)
        keep, add = keep * inverse, add * inverse
        valid = lax.broadcasted_iota(jnp.int32, (32, HD), 0) + holder * 32 < count
        for h in range(8):
            lanes = slice(h * HD, (h + 1) * HD)
            far = far_in[holder // SIDE, holder % SIDE, :, lanes].astype(jnp.float32)
            result = self_out[h, here] * keep[:, h : h + 1] + far * add[:, h : h + 1]
            o_ref[here, lanes] = jnp.where(valid, result, 0.0).astype(jnp.bfloat16)
        return 0

    lax.fori_loop(0, 16, merge, 0, unroll=2)


def attend(tables, arrays):
    vmem, smem = pl.BlockSpec(memory_space=pltpu.VMEM), pl.BlockSpec(memory_space=pltpu.SMEM)
    dma, bf16, f32 = pltpu.SemaphoreType.DMA, jnp.bfloat16, jnp.float32
    flat = (SIDE, SIDE, 32, 1024)
    exchange_sems = [dma((2, 3, 2))] * 4 + [dma((2, 2))]
    return pl.pallas_call(
        attention_kernel,
        out_shape=jax.ShapeDtypeStruct((512, 1024), bf16),
        in_specs=[smem] * len(tables) + [vmem] * len(arrays),
        out_specs=vmem,
        scratch_shapes=[
            pltpu.VMEM((SIDE, SIDE, 2, CAP, 64, 128), bf16),
            pltpu.VMEM((SIDE, SIDE, 2, CAP, 64, 128), bf16),
            pltpu.VMEM((2, SIDE, SIDE, CAP, 64, 128), bf16),
            pltpu.VMEM((2, 2, 2, SIDE, 2, 64, 128), bf16),
            pltpu.VMEM(flat, bf16),
            pltpu.VMEM((2, SIDE, SIDE, 32, 512), bf16),
            pltpu.VMEM((2, 2, 2, SIDE, 32, 256), bf16),
            pltpu.VMEM(flat, bf16),
            pltpu.VMEM((2, SIDE, SIDE, 32, 512), bf16),
            pltpu.VMEM((2, 2, 2, SIDE, 32, 256), bf16),
            pltpu.VMEM((16, 8, 128), f32),
            pltpu.VMEM((16, 8, 128), f32),
            pltpu.VMEM((2, 2, 64, 512), bf16),
            pltpu.VMEM((8, 512, HD), f32),
            pltpu.VMEM((512, HD), f32),
            pltpu.VMEM((512, HD), f32),
            pltpu.VMEM((2, 2, 64, 1024), bf16),
            pltpu.VMEM((16, 2, 2, 2, 64, 1024), bf16),
            pltpu.VMEM((16, HD, 256), bf16),
            pltpu.VMEM((2, 2, 1024, HD), bf16),
            pltpu.VMEM((2, 2, HD + 16, 1024), bf16),
            pltpu.VMEM((2, 6, HD + 8, 256), f32),
            pltpu.VMEM((2, 6, 8, 256), f32),
            pltpu.VMEM((16, HD + 8, 256), f32),
            pltpu.VMEM((16, 8, 256), f32),
            dma((1,)),
            dma((8,)),
            dma((16,)),
            dma((16,)),
            dma((2,)),
            *exchange_sems,
            *exchange_sems,
            *exchange_sems,
            dma((16,)),
            dma((16,)),
            dma((2,)),
            dma((2,)),
            dma((2,)),
        ],
        compiler_params=pltpu.CompilerParams(collective_id=1, has_side_effects=True, vmem_limit_bytes=50 * MIB),
    )(*tables, *arrays)


def body(queries, new_keys, new_values, key_cache, value_cache, page_owner, page_slot, tile_req, tile_node, suffix_len):
    dp_size = lax.axis_size("dp")
    dp_index = lax.axis_index("dp")
    owners = page_owner.reshape(dp_size, 16)
    slot_ids = page_slot.reshape(dp_size, 16)
    order = jnp.arange(16)
    same = owners[:, :, None] == owners[:, None, :]
    rank = jnp.sum(same & (order[None, :] < order[:, None])[None], axis=2, dtype=jnp.int32)
    chosen = (owners[:, :, None] == dp_index) & (rank[:, :, None] == jnp.arange(CAP)[None, None, :])
    picked = jnp.sum(jnp.where(chosen, slot_ids[:, :, None], 0), axis=1, dtype=jnp.int32).reshape(-1)
    my_owner = lax.dynamic_index_in_dim(owners, dp_index, 0, keepdims=False)
    my_rank = lax.dynamic_index_in_dim(rank, dp_index, 0, keepdims=False)
    entries = jnp.concatenate([my_owner // SIDE, my_owner % SIDE, my_rank])
    requests = tile_req.reshape(dp_size, 6)
    nodes = tile_node.reshape(dp_size, 6) - 2 * jnp.arange(dp_size, dtype=jnp.int32)[:, None]
    tiles = jnp.concatenate([requests, nodes], axis=1).reshape(-1)
    hits = requests[:, None, :] == jnp.arange(16)[None, :, None]
    slots = jnp.sum(jnp.where(hits, jnp.arange(6)[None, None, :], 0), axis=2)
    named = jnp.any(hits, axis=2)
    slots = jnp.concatenate([slots.astype(jnp.int32), named.astype(jnp.int32)], axis=1).reshape(-1)
    arrays = (
        jnp.swapaxes(key_cache, 1, 2),
        jnp.swapaxes(value_cache, 1, 2),
        queries.reshape(SIDE, SIDE, 32, 1024),
        new_keys[0].T,
        new_values[0].T,
    )
    return attend((picked, entries, tiles, slots, suffix_len), arrays)[None]


def solution(mesh):
    cut = P("dp", None, "tensor")
    return jax.shard_map(
        body,
        mesh=mesh,
        in_specs=(cut, cut, cut, cut, cut, P(), P(), P(), P(), P("dp")),
        out_specs=cut,
        check_vma=False,
    )
```
